128 devices in a mesh: dp: 8 (over y, z_lo), rec: 16 (over x, z_hi, core).
Axes of the slice: x: 4, y: 4, z: 4 (z_hi: 2, z_lo: 2; z = z_hi * 2 + z_lo), core: 2. Of those that a mesh axis runs over, the one named last changes fastest.
Arguments:
- grad_parts: float32 [8, 16, 512, 7168], P('dp', 'rec'), may hold values from -6 to 6
- params: float32 [16, 512, 7168], P('rec', 'dp'), may hold values from -6 to 6
- first_moment: float32 [16, 512, 7168], P('rec', 'dp'), may hold values from -4 to 4
- second_moment: float32 [16, 512, 7168], P('rec', 'dp'), may hold values from 0.01 to 1
- generator: float32 [4, 16], replicated, may hold values from -1 to 1
Outputs:
- new_params: float32 [16, 512, 7168], P('rec', 'dp')
- new_first: float32 [16, 512, 7168], P('rec', 'dp')
- new_second: float32 [16, 512, 7168], P('rec', 'dp')
- parity: float32 [8, 16, 3, 16, 7168], P('dp', 'rec')
The draws below stay inside these ranges and needn't reach their ends.
All inputs are finite; a program needn't handle non-finite values.
Results may differ from the reference program's by a relative error of at most 0.000098.
Values sent between devices are 32-bit elements; how exact they have to be, the bound alone decides.
A program may use at most 192 MiB of HBM per device.

```python
import math
import jax
import jax.numpy as jnp
from jax import lax

D = 7168
GEN_ROWS = 4
ROWS_REC = 512
PROWS = 16
N_DP = 8
N_REC = 16


def with_spikes(values, rng, source, target, shards_of, factor):
    owner, partner = [(jnp.arange(values.shape[axis_at]) // (values.shape[axis_at] // shards_of)).reshape([-1 if axis == axis_at else 1 for axis in range(values.ndim)]) for axis_at in (source, target)]
    chosen = jax.random.permutation(rng, shards_of)[partner]
    strong = (owner == chosen) | (owner == (partner + shards_of // 2) % shards_of)
    return jnp.where(strong, factor * values, values)


def block_levels(rng, extent, pieces, smallest, high):
    factor_of = 1.0
    for position, parts in pieces:
        heights = jax.random.uniform(jax.random.fold_in(jax.random.fold_in(rng, 6), position), (parts,), jnp.float32, smallest / len(pieces), high / len(pieces))
        factor_of = factor_of * jnp.repeat(jnp.exp(heights), extent[position] // parts).reshape((-1,) + (1,) * (len(extent) - 1 - position))
    return factor_of


def noise(stream_key, shape, deviation, limit, pieces=(), kind=jnp.bfloat16):
    factor_of = block_levels(stream_key, shape, pieces, -0.22, 0.18) if pieces else 1.0
    drawn = jax.random.normal(stream_key, shape, jnp.float32) * deviation * factor_of
    return jnp.minimum(jnp.maximum(drawn, -limit), limit).astype(kind)


def bell_draw_with(stream_key, shape, scale, bound, cuts, heavy, dtype=jnp.bfloat16):
    values = scale * jax.random.normal(stream_key, shape, jnp.float32)
    if cuts:
        values = values * block_levels(stream_key, shape, cuts, -0.22, 0.18)
    return jnp.clip(with_spikes(values, jax.random.fold_in(stream_key, 3), *heavy), -bound, bound).astype(dtype)


def setup_inputs(seed: int = 0) -> dict:
    seeds = jax.random.split(jax.random.key(seed), 6)
    return {
        "grad_parts": bell_draw_with(seeds[0], (N_DP, N_REC, ROWS_REC, D), 0.35, 6.0, ((0, 8), (1, 16)), (0, 2, 8, 2.0), jnp.float32),
        "params": noise(seeds[1], (N_REC, ROWS_REC, D), 1.0, 6.0, ((0, 16), (1, 8)), jnp.float32),
        "first_moment": noise(seeds[2], (N_REC, ROWS_REC, D), 0.3, 4.0, ((0, 16), (1, 8)), jnp.float32),
        "second_moment": jnp.clip(jnp.exp(math.log(1.0) - 4.6051702 * jax.random.uniform(seeds[3], (N_REC, ROWS_REC, D), jnp.float32) ** block_levels(seeds[3], (N_REC, ROWS_REC, D), ((0, 16), (1, 8)), -0.2, 0.2)), 0.01, 1.0),
        "generator": jnp.clip(jax.random.uniform(seeds[4], (GEN_ROWS, N_REC), jnp.float32, -1.0, 1.0), -1.0, 1.0),
    }


def reference(grad_parts, params, first_moment, second_moment, generator):
    grad = lax.optimization_barrier(jnp.sum(grad_parts, axis=0))
    new_first = 0.9 * first_moment + 0.1 * grad
    new_second = 0.999 * second_moment + 0.001 * grad * grad
    bias_one = 1.0 - 0.9 ** 10
    bias_two = 1.0 - 0.999 ** 10
    step_dir = new_first / bias_one / (jnp.sqrt(new_second / bias_two) + 1e-08) + 0.1 * params
    new_params = params - 0.001 * step_dir
    owners = N_REC // GEN_ROWS
    diffs = jnp.stack([step_dir, grad - first_moment, grad * grad - second_moment], axis=0)
    diffs = diffs.reshape(3, N_REC, N_DP, owners, PROWS, D)
    parity = jnp.einsum('ji,kidqrc->djqkrc', generator, diffs, precision=lax.Precision.HIGHEST)
    parity = parity.reshape(N_DP, N_REC, 3, PROWS, D)
    return (new_params, new_first, new_second, parity)
```

```python
import functools

import jax
import jax.numpy as jnp
from jax import lax
from jax.experimental import pallas as pl
from jax.experimental.pallas import tpu as pltpu
from jax.sharding import PartitionSpec as P

MESH = pl.DeviceIdType.MESH
WIDTH = 256
AHEAD = 3

RELAY_UP, RELAY_DOWN, DIRECT_UP, DIRECT_DOWN, SECOND_UP, SECOND_DOWN = range(6)
ZL, CORE, X, ZH = 6, 7, 8, 14
SLOTS = 15


def kernel(
    chunks, width,
    g_ref, p_ref, m_ref, v_ref, gen_ref,
    np_ref, nm_ref, nv_ref, par_ref,
    own, up, down, yr, zr, pmv, dif, cr, wgt, xr, hr,
    ssem, rsem, lsem, osem,
):
    dp = lax.axis_index("dp")
    rec = lax.axis_index("rec")
    y, zl = dp // 2, dp % 2
    x, zh, core = rec // 4, (rec // 2) % 2, rec % 2
    y_up, y_down, y_far = (y + 1) % 4, (y + 3) % 4, (y + 2) % 4
    x_up, x_down, x_far = (x + 1) % 4, (x + 3) % 4, (x + 2) % 4
    to_y_up = (y_up * 2 + zl, rec)
    to_y_down = (y_down * 2 + zl, rec)
    to_zl = (y * 2 + 1 - zl, rec)
    to_core = (dp, x * 4 + zh * 2 + 1 - core)
    to_zh = (dp, x * 4 + (1 - zh) * 2 + core)
    to_x_up = (dp, x_up * 4 + zh * 2 + core)
    to_x_down = (dp, x_down * 4 + zh * 2 + core)

    barrier = pltpu.get_barrier_semaphore()
    peers = (to_y_up, to_y_down, to_zl, to_core, to_zh, to_x_up, to_x_down)
    for peer in peers:
        pl.semaphore_signal(barrier, inc=1, device_id=peer, device_id_type=MESH)
    pl.semaphore_wait(barrier, len(peers))

    def cols(k):
        return pl.ds(pl.multiple_of(k * width, width), width)

    def remote(k, slot, src, dst, device):
        return pltpu.make_async_remote_copy(
            src_ref=src, dst_ref=dst, send_sem=ssem.at[k, slot], recv_sem=rsem.at[k, slot],
            device_id=device, device_id_type=MESH,
        )

    def y_copy(k, slot):
        def rows(block, half):
            return g_ref.at[0, 0, pl.ds(pl.multiple_of(block * 128 + half * 64, 64), 64), cols(k)]

        src = {
            RELAY_UP: lambda: rows(y_far, 0),
            RELAY_DOWN: lambda: rows(y_far, 1),
            DIRECT_UP: lambda: rows(y_up, 1),
            DIRECT_DOWN: lambda: rows(y_down, 0),
            SECOND_UP: lambda: yr.at[k, RELAY_UP],
            SECOND_DOWN: lambda: yr.at[k, RELAY_DOWN],
        }[slot]()
        return remote(k, slot, src, yr.at[k, slot], to_y_up if slot % 2 == 0 else to_y_down)

    def x_copy(k, slot):
        src = {
            RELAY_UP: lambda: wgt.at[k, x_far, 0],
            RELAY_DOWN: lambda: wgt.at[k, x_far, 1],
            DIRECT_UP: lambda: wgt.at[k, x_up, 1],
            DIRECT_DOWN: lambda: wgt.at[k, x_down, 0],
            SECOND_UP: lambda: xr.at[k, RELAY_UP],
            SECOND_DOWN: lambda: xr.at[k, RELAY_DOWN],
        }[slot]()
        return remote(k, X + slot, src, xr.at[k, slot], to_x_up if slot % 2 == 0 else to_x_down)

    def zl_copy(k):
        return remote(k, ZL, own.at[k, 1 - zl], zr.at[k], to_zl)

    def core_copy(k):
        return remote(k, CORE, dif.at[k, 1 - core], cr.at[k], to_core)

    def zh_copy(k):
        return remote(k, ZH, wgt.at[k, x, 1 - zh], hr.at[k], to_zh)

    def recv_done(k, slot, buf):
        remote(k, slot, buf, buf, to_core).wait_recv()

    def load(k, i):
        def rows(block, half, n):
            return g_ref.at[0, 0, pl.ds(pl.multiple_of(block * 128 + half * 64, 64), n), cols(k)]

        src, dst = (
            lambda: (rows(y_up, 0, 64), up.at[k]),
            lambda: (rows(y_down, 1, 64), down.at[k]),
            lambda: (rows(y, 0, 64), own.at[k, 0]),
            lambda: (rows(y, 1, 64), own.at[k, 1]),
            lambda: (p_ref.at[0, :, cols(k)], pmv.at[k, 0]),
            lambda: (m_ref.at[0, :, cols(k)], pmv.at[k, 1]),
            lambda: (v_ref.at[0, :, cols(k)], pmv.at[k, 2]),
        )[i]()
        return pltpu.make_async_copy(src, dst, lsem.at[k, i])

    def store(k, i):
        src, dst = (
            lambda: (pmv.at[k, 0], np_ref.at[0, :, cols(k)]),
            lambda: (pmv.at[k, 1], nm_ref.at[0, :, cols(k)]),
            lambda: (pmv.at[k, 2], nv_ref.at[0, :, cols(k)]),
            lambda: (wgt.at[k, x, zh], par_ref.at[0, 0, :, :, cols(k)]),
        )[i]()
        return pltpu.make_async_copy(src, dst, osem.at[k, i])

    def begin(k):
        for slot in (RELAY_UP, RELAY_DOWN, DIRECT_UP, DIRECT_DOWN):
            y_copy(k, slot).start()
        for i in range(7):
            load(k, i).start()

    def y_relay(k):
        for slot, mine, i, onward in ((RELAY_UP, up, 0, SECOND_UP), (RELAY_DOWN, down, 1, SECOND_DOWN)):
            load(k, i).wait()
            recv_done(k, slot, yr.at[k, slot])
            yr[k, slot] = yr[k, slot] + mine[k]
            y_copy(k, onward).start()

    def y_half(k, half):
        pltpu.make_async_copy(own.at[k, half], own.at[k, half], lsem.at[k, 2 + half]).wait()
        recv_done(k, 3 - half, yr.at[k, 3 - half])
        recv_done(k, 4 + half, yr.at[k, 4 + half])
        own[k, half] = own[k, half] + yr[k, 3 - half] + yr[k, 4 + half]

    def y_final(k):
        y_half(k, 1 - zl)
        zl_copy(k).start()
        y_half(k, zl)

    def adam(k):
        for i in (4, 5, 6):
            load(k, i).wait()
        recv_done(k, ZL, zr.at[k])
        bias_one = 1.0 - 0.9**10
        bias_two = 1.0 - 0.999**10
        for q in range(4):
            r = pl.ds(q * 16, 16)
            grad = own[k, zl, r] + zr[k, r]
            params, first, second = pmv[k, 0, r], pmv[k, 1, r], pmv[k, 2, r]
            square = grad * grad
            new_first = 0.9 * first + 0.1 * grad
            new_second = 0.999 * second + 0.001 * square
            step = new_first / bias_one / (jnp.sqrt(new_second / bias_two) + 1e-08) + 0.1 * params
            dif[k, q % 2, q // 2, 0] = step
            dif[k, q % 2, q // 2, 1] = grad - first
            dif[k, q % 2, q // 2, 2] = square - second
            pmv[k, 0, r] = params - 0.001 * step
            pmv[k, 1, r] = new_first
            pmv[k, 2, r] = new_second
        core_copy(k).start()
        for i in range(3):
            store(k, i).start()

    def weigh(k):
        recv_done(k, CORE, cr.at[k])
        for half in range(2):
            mine = dif[k, core, half]
            other = cr[k, half]
            for j in range(4):
                a = gen_ref[j, rec]
                b = gen_ref[j, rec + 1 - 2 * core]
                wgt[k, j, half] = a * mine + b * other
        for slot in (RELAY_UP, RELAY_DOWN, DIRECT_UP, DIRECT_DOWN):
            x_copy(k, slot).start()

    def x_relay(k):
        for slot, block, half, onward in ((RELAY_UP, x_up, 0, SECOND_UP), (RELAY_DOWN, x_down, 1, SECOND_DOWN)):
            recv_done(k, X + slot, xr.at[k, slot])
            xr[k, slot] = xr[k, slot] + wgt[k, block, half]
            x_copy(k, onward).start()

    def x_half(k, half):
        recv_done(k, X + 3 - half, xr.at[k, 3 - half])
        recv_done(k, X + 4 + half, xr.at[k, 4 + half])
        wgt[k, x, half] = wgt[k, x, half] + xr[k, 3 - half] + xr[k, 4 + half]

    def x_final(k):
        x_half(k, 1 - zh)
        zh_copy(k).start()
        x_half(k, zh)

    def finish(k):
        recv_done(k, ZH, hr.at[k])
        wgt[k, x, zh] = wgt[k, x, zh] + hr[k]
        store(k, 3).start()

    for k in range(AHEAD):
        begin(k)

    stages = (y_relay, y_final, adam, weigh, x_relay, x_final, finish)

    def body(t, carry):
        @pl.when(t + AHEAD < chunks)
        def _():
            begin(t + AHEAD)

        for lag, stage in enumerate(stages):
            @pl.when(jnp.logical_and(t >= lag, t - lag < chunks))
            def _(stage=stage, lag=lag):
                stage(t - lag)

        return carry

    lax.fori_loop(0, chunks + len(stages) - 1, body, 0)

    def drain(k, carry):
        for slot in range(6):
            y_copy(k, slot).wait_send()
            x_copy(k, slot).wait_send()
        zl_copy(k).wait_send()
        core_copy(k).wait_send()
        zh_copy(k).wait_send()
        for i in range(4):
            store(k, i).wait()
        return carry

    lax.fori_loop(0, chunks, drain, 0)


def per_device(grad_parts, params, first_moment, second_moment, generator):
    width_all = params.shape[2]
    width = WIDTH
    chunks = width_all // width
    any_spec = pl.BlockSpec(memory_space=pl.ANY)
    f32 = jnp.float32
    return pl.pallas_call(
        functools.partial(kernel, chunks, width),
        out_shape=(
            jax.ShapeDtypeStruct(params.shape, f32),
            jax.ShapeDtypeStruct(params.shape, f32),
            jax.ShapeDtypeStruct(params.shape, f32),
            jax.ShapeDtypeStruct((1, 1, 3, 16, width_all), f32),
        ),
        in_specs=[any_spec] * 4 + [pl.BlockSpec(memory_space=pltpu.SMEM)],
        out_specs=(any_spec,) * 4,
        scratch_shapes=[
            pltpu.VMEM((chunks, 2, 64, width), f32),
            pltpu.VMEM((chunks, 64, width), f32),
            pltpu.VMEM((chunks, 64, width), f32),
            pltpu.VMEM((chunks, 6, 64, width), f32),
            pltpu.VMEM((chunks, 64, width), f32),
            pltpu.VMEM((chunks, 3, 64, width), f32),
            pltpu.VMEM((chunks, 2, 2, 3, 16, width), f32),
            pltpu.VMEM((chunks, 2, 3, 16, width), f32),
            pltpu.VMEM((chunks, 4, 2, 3, 16, width), f32),
            pltpu.VMEM((chunks, 6, 3, 16, width), f32),
            pltpu.VMEM((chunks, 3, 16, width), f32),
            pltpu.SemaphoreType.DMA((chunks, SLOTS)),
            pltpu.SemaphoreType.DMA((chunks, SLOTS)),
            pltpu.SemaphoreType.DMA((chunks, 7)),
            pltpu.SemaphoreType.DMA((chunks, 4)),
        ],
        compiler_params=pltpu.CompilerParams(
            collective_id=0, has_side_effects=True, vmem_limit_bytes=60 << 20
        ),
        cost_estimate=pl.CostEstimate(
            flops=100_000_000, bytes_accessed=60_000_000, transcendentals=458_752
        ),
    )(grad_parts, params, first_moment, second_moment, generator)


def solution(mesh):
    in_specs = (
        P("dp", "rec", None, None),
        P("rec", "dp", None),
        P("rec", "dp", None),
        P("rec", "dp", None),
        P(),
    )
    out_specs = (
        P("rec", "dp", None),
        P("rec", "dp", None),
        P("rec", "dp", None),
        P("dp", "rec", None, None, None),
    )
    return jax.shard_map(
        per_device, mesh=mesh, in_specs=in_specs, out_specs=out_specs, check_vma=False
    )
```

```python
import functools

import jax
import jax.numpy as jnp
from jax import lax
from jax.experimental import pallas as pl
from jax.experimental.pallas import tpu as pltpu
from jax.sharding import PartitionSpec as P

MESH = pl.DeviceIdType.MESH
TILE = 128

CHUNKS = (
    (True, False, 6), (True, False, 6), (False, False, 6), (False, False, 6), (False, False, 2),
    (False, False, 5), (False, False, 5), (False, False, 5), (False, False, 5), (False, False, 3),
    (False, False, 1), (False, False, 2), (False, False, 2), (False, False, 1), (False, False, 1),
)
BEGIN, ZSUM, YRELAY, YFINAL, ADAM, WEIGH, XRELAY, XFINAL, FINISH = range(9)
ORDER = (
    (BEGIN, 0), (BEGIN, 2), (YRELAY, 2), (BEGIN, 3), (YFINAL, 2), (ZSUM, 0),
    (YRELAY, 3), (BEGIN, 1), (ADAM, 2), (YRELAY, 0), (WEIGH, 2), (BEGIN, 4),
    (XRELAY, 2), (YFINAL, 3), (BEGIN, 5), (ADAM, 0), (YRELAY, 4), (WEIGH, 0),
    (XFINAL, 2), (ZSUM, 1), (YRELAY, 5), (XRELAY, 0), (ADAM, 3), (YFINAL, 4),
    (WEIGH, 3), (YRELAY, 1), (XFINAL, 0), (FINISH, 2), (ADAM, 4), (BEGIN, 6),
    (XRELAY, 3), (YFINAL, 5), (WEIGH, 4), (ADAM, 1), (WEIGH, 1), (XFINAL, 3),
    (YRELAY, 6), (FINISH, 0), (XRELAY, 4), (ADAM, 5), (BEGIN, 7), (XRELAY, 1),
    (WEIGH, 5), (YFINAL, 6), (XFINAL, 4), (FINISH, 3), (YRELAY, 7), (XFINAL, 1),
    (ADAM, 6), (BEGIN, 8), (XRELAY, 5), (WEIGH, 6), (FINISH, 4), (YFINAL, 7),
    (XFINAL, 5), (YRELAY, 8), (FINISH, 1), (XRELAY, 6), (BEGIN, 9), (ADAM, 7),
    (WEIGH, 7), (YFINAL, 8), (XFINAL, 6), (BEGIN, 10), (YRELAY, 9), (FINISH, 5),
    (BEGIN, 11), (XRELAY, 7), (YRELAY, 10), (ADAM, 8), (YFINAL, 9), (BEGIN, 12),
    (WEIGH, 8), (YRELAY, 11), (XFINAL, 7), (YFINAL, 10), (FINISH, 6), (BEGIN, 13),
    (YRELAY, 12), (ADAM, 9), (XRELAY, 8), (BEGIN, 14), (WEIGH, 9), (YFINAL, 11),
    (YRELAY, 13), (YFINAL, 12), (XFINAL, 8), (YRELAY, 14), (FINISH, 7), (ADAM, 10),
    (XRELAY, 9), (YFINAL, 13), (ADAM, 11), (WEIGH, 10), (YFINAL, 14), (ADAM, 12),
    (WEIGH, 11), (WEIGH, 12), (XFINAL, 9), (XRELAY, 10), (XRELAY, 11), (FINISH, 8),
    (ADAM, 13), (XRELAY, 12), (ADAM, 14), (WEIGH, 13), (XFINAL, 10), (WEIGH, 14),
    (XFINAL, 11), (XFINAL, 12), (XRELAY, 13), (FINISH, 9), (XRELAY, 14), (FINISH, 10),
    (XFINAL, 13), (FINISH, 11), (XFINAL, 14), (FINISH, 12), (FINISH, 13), (FINISH, 14),
)

RELAY_UP, RELAY_DOWN, DIRECT_UP, DIRECT_DOWN, SECOND_UP, SECOND_DOWN = range(6)
Z_LO, CORE, X_RING, Z_HI, Z_HI_CORE = 6, 7, 8, 14, 15
SLOTS = 16
LOADS = 6


def kernel(
    g_ref, p_ref, m_ref, v_ref, gen_ref,
    np_ref, nm_ref, nv_ref, par_ref,
    own, got, dif, cr, wgt, xr, hr,
    ssem, rsem, lsem,
):
    dp = lax.axis_index("dp")
    rec = lax.axis_index("rec")
    y, zl = dp // 2, dp % 2
    x, zh, core = rec // 4, (rec // 2) % 2, rec % 2
    y_up, y_down, y_far = (y + 1) % 4, (y + 3) % 4, (y + 2) % 4
    x_up, x_down, x_far = (x + 1) % 4, (x + 3) % 4, (x + 2) % 4
    to_y_up = (y_up * 2 + zl, rec)
    to_y_down = (y_down * 2 + zl, rec)
    to_zl = (y * 2 + 1 - zl, rec)
    rec_core = x * 4 + zh * 2 + 1 - core
    rec_zh = x * 4 + (1 - zh) * 2 + core
    rec_both = x * 4 + (1 - zh) * 2 + 1 - core
    to_core, to_zh, to_both = (dp, rec_core), (dp, rec_zh), (dp, rec_both)
    to_x_up = (dp, x_up * 4 + zh * 2 + core)
    to_x_down = (dp, x_down * 4 + zh * 2 + core)

    barrier = pltpu.get_barrier_semaphore()
    peers = (to_y_up, to_y_down, to_zl, to_core, to_zh, to_both, to_x_up, to_x_down)
    for peer in peers:
        pl.semaphore_signal(barrier, inc=1, device_id=peer, device_id_type=MESH)
    pl.semaphore_wait(barrier, len(peers))

    starts = []
    for _, _, tiles in CHUNKS:
        starts.append(starts[-1] + last if starts else 0)
        last = tiles * TILE

    def cols(k):
        return pl.ds(starts[k], CHUNKS[k][2] * TILE)

    def over_cols(k, work):
        start, tiles = starts[k], CHUNKS[k][2]
        step = 2 * TILE if tiles % 2 == 0 else TILE
        n = tiles * TILE // step
        if n == 1:
            work(pl.ds(start, step))
        else:
            def body(i, carry):
                work(pl.ds(pl.multiple_of(start + i * step, TILE), step))
                return carry

            lax.fori_loop(0, n, body, 0)

    def remote(k, slot, src, dst, device):
        return pltpu.make_async_remote_copy(
            src_ref=src, dst_ref=dst, send_sem=ssem.at[k, slot], recv_sem=rsem.at[k, slot],
            device_id=device, device_id_type=MESH,
        )

    def z_first(k):
        return CHUNKS[k][0]

    def early(k):
        return CHUNKS[k][1]

    def y_place(k, slot):
        return (4 + slot // 2, (slot % 2) * 32, 32) if z_first(k) else (slot, 0, 64)

    def y_in(k, slot):
        i, r, n = y_place(k, slot)
        return got.at[i, pl.ds(r, n), cols(k)]

    def y_copy(k, slot):
        def part(block, half):
            if z_first(k):
                return got.at[block, pl.ds(half * 32, 32), cols(k)]
            return g_ref.at[block, half, :, cols(k)]

        src = {
            RELAY_UP: lambda: part(y_far, 0),
            RELAY_DOWN: lambda: part(y_far, 1),
            DIRECT_UP: lambda: part(y_up, 1),
            DIRECT_DOWN: lambda: part(y_down, 0),
            SECOND_UP: lambda: y_in(k, RELAY_UP),
            SECOND_DOWN: lambda: y_in(k, RELAY_DOWN),
        }[slot]()
        return remote(k, slot, src, y_in(k, slot), to_y_up if slot % 2 == 0 else to_y_down)

    def zl_copy(k):
        if z_first(k):
            return remote(k, Z_LO, g_ref.at[:, 1 - zl, :, cols(k)], got.at[0:4, :, cols(k)], to_zl)
        return remote(k, Z_LO, own.at[1 - zl, :, cols(k)], got.at[6, :, cols(k)], to_zl)

    def group_copies(k):
        if early(k):
            return (
                remote(k, Z_HI_CORE, dif.at[1 - core, 1 - zh, :, :, cols(k)], cr.at[1, :, :, cols(k)], to_both),
                remote(k, Z_HI, dif.at[core, 1 - zh, :, :, cols(k)], hr.at[:, :, cols(k)], to_zh),
                remote(k, CORE, dif.at[1 - core, zh, :, :, cols(k)], cr.at[0, :, :, cols(k)], to_core),
            )
        return (remote(k, CORE, dif.at[1 - core, :, :, :, cols(k)], cr.at[:, :, :, cols(k)], to_core),)

    def x_part(k, block, half):
        if early(k):
            return wgt.at[block, 0, :, pl.ds(half * 8, 8), cols(k)]
        return wgt.at[block, half, :, :, cols(k)]

    def x_in(k, slot):
        return xr.at[slot, :, pl.ds(0, 8 if early(k) else 16), cols(k)]

    def x_copy(k, slot):
        src = {
            RELAY_UP: lambda: x_part(k, x_far, 0),
            RELAY_DOWN: lambda: x_part(k, x_far, 1),
            DIRECT_UP: lambda: x_part(k, x_up, 1),
            DIRECT_DOWN: lambda: x_part(k, x_down, 0),
            SECOND_UP: lambda: x_in(k, RELAY_UP),
            SECOND_DOWN: lambda: x_in(k, RELAY_DOWN),
        }[slot]()
        return remote(k, X_RING + slot, src, x_in(k, slot), to_x_up if slot % 2 == 0 else to_x_down)

    def zh_copy(k):
        return remote(k, Z_HI, wgt.at[x, 1 - zh, :, :, cols(k)], hr.at[:, :, cols(k)], to_zh)

    def arrived(k, slot, buf):
        remote(k, slot, buf, buf, to_core).wait_recv()

    def loads(k):
        c = cols(k)
        if z_first(k):
            pairs = [(g_ref.at[:, zl, :, c], own.at[:, :, c])]
        else:
            pairs = [
                (g_ref.at[y_up, 0, :, c], own.at[2, :, c]),
                (g_ref.at[y_down, 1, :, c], own.at[3, :, c]),
                (g_ref.at[y, :, :, c], own.at[0:2, :, c]),
            ]
        state = ((p_ref, np_ref), (m_ref, nm_ref), (v_ref, nv_ref))
        pairs += [(src.at[0, :, c], dst.at[0, :, c]) for src, dst in state]
        return [functools.partial(pltpu.make_async_copy, src, dst, lsem.at[k, i]) for i, (src, dst) in enumerate(pairs)]

    def begin(k):
        if z_first(k):
            zl_copy(k).start()
        else:
            for slot in (RELAY_UP, RELAY_DOWN, DIRECT_UP, DIRECT_DOWN):
                y_copy(k, slot).start()
        for copy in loads(k):
            copy().start()

    def zsum(k):
        loads(k)[0]().wait()
        arrived(k, Z_LO, got.at[0:4, :, cols(k)])

        def add(block):
            def work(c):
                got[block, :, c] = got[block, :, c] + own[block, :, c]

            over_cols(k, work)

        add(y_far)
        y_copy(k, RELAY_UP).start()
        y_copy(k, RELAY_DOWN).start()
        add(y_up)
        y_copy(k, DIRECT_UP).start()
        add(y_down)
        y_copy(k, DIRECT_DOWN).start()
        add(y)

    def yrelay(k):
        for slot, block, onward in ((RELAY_UP, y_up, SECOND_UP), (RELAY_DOWN, y_down, SECOND_DOWN)):
            if not z_first(k):
                loads(k)[slot]().wait()
            arrived(k, slot, y_in(k, slot))
            i, r, n = y_place(k, slot)

            def work(c):
                if z_first(k):
                    mine = got[block, pl.ds(slot * 32, 32), c]
                else:
                    mine = own[2 + slot, :, c]
                got[i, pl.ds(r, n), c] = got[i, pl.ds(r, n), c] + mine

            over_cols(k, work)
            y_copy(k, onward).start()

    def yfinal(k):
        loads(k)[2]().wait()
        for turn, half in enumerate((1 - zl, zl)):
            for slot in (3 - half, 4 + half):
                arrived(k, slot, got.at[slot, :, cols(k)])

            def work(c):
                own[half, :, c] = own[half, :, c] + got[3 - half, :, c] + got[4 + half, :, c]

            over_cols(k, work)
            if turn == 0:
                zl_copy(k).start()

    def adam(k):
        for copy in loads(k)[-3:]:
            copy().wait()
        if z_first(k):
            for slot in (DIRECT_DOWN, SECOND_UP, DIRECT_UP, SECOND_DOWN):
                arrived(k, slot, y_in(k, slot))
        else:
            arrived(k, Z_LO, got.at[6, :, cols(k)])
        bias_one = 1.0 - 0.9**10
        bias_two = 1.0 - 0.999**10

        def work(c):
            for q in range(4):
                r = pl.ds(q * 16, 16)
                if z_first(k):
                    grad = got[y, r, c]
                    for slot in ((DIRECT_DOWN, SECOND_UP) if q < 2 else (DIRECT_UP, SECOND_DOWN)):
                        i, first_row, _ = y_place(k, slot)
                        grad = grad + got[i, pl.ds(first_row + (q % 2) * 16, 16), c]
                else:
                    grad = own[zl, r, c] + got[6, r, c]
                params, first, second = np_ref[0, r, c], nm_ref[0, r, c], nv_ref[0, r, c]
                square = grad * grad
                new_first = 0.9 * first + 0.1 * grad
                new_second = 0.999 * second + 0.001 * square
                step = new_first / bias_one / (jnp.sqrt(new_second / bias_two) + 1e-08) + 0.1 * params
                dif[q % 2, q // 2, 0, :, c] = step
                dif[q % 2, q // 2, 1, :, c] = grad - first
                dif[q % 2, q // 2, 2, :, c] = square - second
                np_ref[0, r, c] = params - 0.001 * step
                nm_ref[0, r, c] = new_first
                nv_ref[0, r, c] = new_second

        over_cols(k, work)
        for copy in group_copies(k):
            copy.start()

    def weigh(k):
        if early(k):
            arrived(k, CORE, cr.at[0, :, :, cols(k)])
            arrived(k, Z_HI, hr.at[:, :, cols(k)])
            arrived(k, Z_HI_CORE, cr.at[1, :, :, cols(k)])
        else:
            arrived(k, CORE, cr.at[:, :, :, cols(k)])

        def work(c):
            if early(k):
                fields = (dif[core, zh, :, :, c], cr[0, :, :, c], hr[:, :, c], cr[1, :, :, c])
                for j in range(4):
                    total = gen_ref[j, rec] * fields[0]
                    for member, field in zip((rec_core, rec_zh, rec_both), fields[1:]):
                        total = total + gen_ref[j, member] * field
                    wgt[j, 0, :, :, c] = total
            else:
                for half in range(2):
                    mine, other = dif[core, half, :, :, c], cr[half, :, :, c]
                    for j in range(4):
                        wgt[j, half, :, :, c] = gen_ref[j, rec] * mine + gen_ref[j, rec_core] * other

        over_cols(k, work)
        for slot in (RELAY_UP, RELAY_DOWN, DIRECT_UP, DIRECT_DOWN):
            x_copy(k, slot).start()

    def xrelay(k):
        for slot, block, onward in ((RELAY_UP, x_up, SECOND_UP), (RELAY_DOWN, x_down, SECOND_DOWN)):
            arrived(k, X_RING + slot, x_in(k, slot))

            def work(c):
                if early(k):
                    r = pl.ds(0, 8)
                    xr[slot, :, r, c] = xr[slot, :, r, c] + wgt[block, 0, :, pl.ds(slot * 8, 8), c]
                else:
                    xr[slot, :, :, c] = xr[slot, :, :, c] + wgt[block, slot, :, :, c]

            over_cols(k, work)
            x_copy(k, onward).start()

    def xfinal(k):
        if early(k):
            for slot in (DIRECT_DOWN, SECOND_UP, DIRECT_UP, SECOND_DOWN):
                arrived(k, X_RING + slot, x_in(k, slot))

            def work(c):
                r = pl.ds(0, 8)
                for half in range(2):
                    h = pl.ds(half * 8, 8)
                    par_ref[0, 0, :, h, c] = wgt[x, 0, :, h, c] + xr[3 - half, :, r, c] + xr[4 + half, :, r, c]

            over_cols(k, work)
            return
        for turn, half in enumerate((1 - zh, zh)):
            for slot in (3 - half, 4 + half):
                arrived(k, X_RING + slot, xr.at[slot, :, :, cols(k)])

            def work(c):
                wgt[x, half, :, :, c] = wgt[x, half, :, :, c] + xr[3 - half, :, :, c] + xr[4 + half, :, :, c]

            over_cols(k, work)
            if turn == 0:
                zh_copy(k).start()

    def finish(k):
        arrived(k, Z_HI, hr.at[:, :, cols(k)])

        def work(c):
            par_ref[0, 0, :, :, c] = wgt[x, zh, :, :, c] + hr[:, :, c]

        over_cols(k, work)

    stages = {
        BEGIN: begin, ZSUM: zsum, YRELAY: yrelay, YFINAL: yfinal, ADAM: adam,
        WEIGH: weigh, XRELAY: xrelay, XFINAL: xfinal, FINISH: finish,
    }
    for stage, k in ORDER:
        stages[stage](k)

    for k in range(len(CHUNKS)):
        for slot in range(6):
            y_copy(k, slot).wait_send()
            x_copy(k, slot).wait_send()
        zl_copy(k).wait_send()
        for copy in group_copies(k):
            copy.wait_send()
        if not early(k):
            zh_copy(k).wait_send()


def copy_out(*refs):
    n = len(refs) // 2
    sems = refs[-1]
    copies = []
    for i in range(4):
        src, dst = refs[i], refs[4 + i]
        for part in range(4):
            if i < 3:
                where = (0, pl.ds(part * 16, 16))
            elif part < 3:
                where = (0, 0, part)
            else:
                continue
            copies.append(pltpu.make_async_copy(src.at[where], dst.at[where], sems.at[i, part]))
    for copy in copies:
        copy.start()
    for copy in copies:
        copy.wait()


def per_device(grad_parts, params, first_moment, second_moment, generator):
    width = params.shape[2]
    assert sum(tiles for _, _, tiles in CHUNKS) * TILE == width
    n = len(CHUNKS)
    any_spec = pl.BlockSpec(memory_space=pl.ANY)
    f32 = jnp.float32
    outs = (jax.ShapeDtypeStruct(params.shape, f32),) * 3 + (jax.ShapeDtypeStruct((1, 1, 3, 16, width), f32),)
    results = pl.pallas_call(
        kernel,
        out_shape=tuple(pltpu.VMEM(out.shape, out.dtype) for out in outs),
        in_specs=[any_spec] * 4 + [pl.BlockSpec(memory_space=pltpu.SMEM)],
        out_specs=(pl.BlockSpec(memory_space=pltpu.VMEM),) * 4,
        scratch_shapes=[
            pltpu.VMEM((4, 64, width), f32),
            pltpu.VMEM((7, 64, width), f32),
            pltpu.VMEM((2, 2, 3, 16, width), f32),
            pltpu.VMEM((2, 3, 16, width), f32),
            pltpu.VMEM((4, 2, 3, 16, width), f32),
            pltpu.VMEM((6, 3, 16, width), f32),
            pltpu.VMEM((3, 16, width), f32),
            pltpu.SemaphoreType.DMA((n, SLOTS)),
            pltpu.SemaphoreType.DMA((n, SLOTS)),
            pltpu.SemaphoreType.DMA((n, LOADS)),
        ],
        compiler_params=pltpu.CompilerParams(
            collective_id=0, has_side_effects=True, vmem_limit_bytes=50 << 20
        ),
        cost_estimate=pl.CostEstimate(
            flops=100_000_000, bytes_accessed=60_000_000, transcendentals=458_752
        ),
        name="adam_parity",
    )(grad_parts.reshape(4, 2, 64, width), params, first_moment, second_moment, generator)
    return pl.pallas_call(
        copy_out,
        out_shape=outs,
        in_specs=[any_spec] * 4,
        out_specs=(any_spec,) * 4,
        scratch_shapes=[pltpu.SemaphoreType.DMA((4, 4))],
        compiler_params=pltpu.CompilerParams(vmem_limit_bytes=1 << 20),
        cost_estimate=pl.CostEstimate(flops=0, bytes_accessed=13_800_000, transcendentals=0),
        name="copy_out",
    )(*results)


def solution(mesh):
    in_specs = (
        P("dp", "rec", None, None),
        P("rec", "dp", None),
        P("rec", "dp", None),
        P("rec", "dp", None),
        P(),
    )
    out_specs = (
        P("rec", "dp", None),
        P("rec", "dp", None),
        P("rec", "dp", None),
        P("dp", "rec", None, None, None),
    )
    return jax.shard_map(
        per_device, mesh=mesh, in_specs=in_specs, out_specs=out_specs, check_vma=False
    )
```

```python
import functools

import jax
import jax.numpy as jnp
from jax import lax
from jax.experimental import pallas as pl
from jax.experimental.pallas import tpu as pltpu
from jax.sharding import PartitionSpec as P

MESH = pl.DeviceIdType.MESH
TILE = 128

CHUNKS = (
    (0, 0, 0, 6), (0, 0, 0, 7), (1, 0, 0, 8), (0, 0, 0, 1), (0, 0, 0, 6), (0, 0, 0, 6), (0, 1, 0, 3),
    (0, 0, 0, 3), (1, 0, 0, 4), (0, 1, 0, 2), (0, 0, 0, 2), (0, 1, 0, 2), (1, 1, 0, 3), (1, 0, 0, 1),
    (1, 1, 1, 2),
)
BEGIN, ZSUM, YRELAY, YFINAL, ADAM, WEIGH, XRELAY, XFINAL, FINISH = range(9)
ORDER = (
    (BEGIN, 2), (BEGIN, 0), (YRELAY, 0), (BEGIN, 1), (YFINAL, 0), (YRELAY, 1),
    (BEGIN, 8), (ZSUM, 2), (ADAM, 0), (YFINAL, 1), (BEGIN, 3), (WEIGH, 0),
    (YRELAY, 2), (YRELAY, 3), (BEGIN, 4), (XRELAY, 0), (ADAM, 2), (BEGIN, 12),
    (YFINAL, 3), (WEIGH, 2), (ADAM, 1), (YRELAY, 4), (XFINAL, 0), (WEIGH, 1),
    (BEGIN, 5), (XRELAY, 2), (BEGIN, 13), (YFINAL, 4), (ADAM, 3), (WEIGH, 3),
    (YRELAY, 5), (FINISH, 0), (XRELAY, 1), (BEGIN, 14), (BEGIN, 6), (ADAM, 4),
    (YFINAL, 5), (BEGIN, 7), (XFINAL, 2), (WEIGH, 4), (YRELAY, 6), (XRELAY, 3),
    (YRELAY, 7), (XFINAL, 1), (ADAM, 5), (ZSUM, 8), (XRELAY, 4), (YFINAL, 6),
    (WEIGH, 5), (BEGIN, 9), (FINISH, 2), (YFINAL, 7), (XFINAL, 3), (YRELAY, 8),
    (FINISH, 1), (XFINAL, 4), (BEGIN, 10), (YRELAY, 9), (ADAM, 6), (XRELAY, 5),
    (ADAM, 8), (ADAM, 7), (BEGIN, 11), (FINISH, 3), (YRELAY, 10), (WEIGH, 8),
    (WEIGH, 7), (YFINAL, 9), (FINISH, 4), (ZSUM, 12), (YRELAY, 11), (XFINAL, 5),
    (WEIGH, 6), (XRELAY, 8), (YFINAL, 10), (ADAM, 9), (ZSUM, 13), (YRELAY, 12),
    (ZSUM, 14), (YFINAL, 11), (XRELAY, 7), (YRELAY, 13), (FINISH, 5), (ADAM, 10),
    (ADAM, 12), (XRELAY, 6), (WEIGH, 10), (WEIGH, 9), (ADAM, 13), (ADAM, 11),
    (ADAM, 14), (XFINAL, 8), (XFINAL, 7), (WEIGH, 13), (XFINAL, 6), (XRELAY, 10),
    (WEIGH, 12), (XRELAY, 9), (XRELAY, 13), (WEIGH, 11), (XFINAL, 10), (XRELAY, 12),
    (WEIGH, 14), (XFINAL, 9), (FINISH, 8), (XFINAL, 13), (XRELAY, 11), (FINISH, 7),
    (XFINAL, 12), (FINISH, 10), (FINISH, 13), (XFINAL, 11), (XFINAL, 14),
)

RELAY_UP, RELAY_DOWN, DIRECT_UP, DIRECT_DOWN, SECOND_UP, SECOND_DOWN = range(6)
TO_UP, TO_DOWN, TO_FAR = range(3)
Z_LO, CORE, X_RING, Z_HI, Z_HI_CORE = 6, 7, 8, 14, 15
SLOTS = 16
LOADS = 6


def kernel(
    g_ref, p_ref, m_ref, v_ref, gen_ref,
    np_ref, nm_ref, nv_ref, par_ref,
    own, got, dif, cr, wgt, xr, hr,
    ssem, rsem, lsem,
):
    dp = lax.axis_index("dp")
    rec = lax.axis_index("rec")
    y, zl = dp // 2, dp % 2
    x, zh, core = rec // 4, (rec // 2) % 2, rec % 2
    y_up, y_down, y_far = (y + 1) % 4, (y + 3) % 4, (y + 2) % 4
    x_up, x_down, x_far = (x + 1) % 4, (x + 3) % 4, (x + 2) % 4
    to_y_up = (y_up * 2 + zl, rec)
    to_y_down = (y_down * 2 + zl, rec)
    to_y_far = (y_far * 2 + zl, rec)
    to_zl = (y * 2 + 1 - zl, rec)
    rec_core = x * 4 + zh * 2 + 1 - core
    rec_zh = x * 4 + (1 - zh) * 2 + core
    rec_both = x * 4 + (1 - zh) * 2 + 1 - core
    to_core, to_zh, to_both = (dp, rec_core), (dp, rec_zh), (dp, rec_both)
    to_x_up = (dp, x_up * 4 + zh * 2 + core)
    to_x_down = (dp, x_down * 4 + zh * 2 + core)

    to_x_far = (dp, x_far * 4 + zh * 2 + core)

    barrier = pltpu.get_barrier_semaphore()
    peers = (to_y_up, to_y_down, to_y_far, to_zl, to_core, to_zh, to_both, to_x_up, to_x_down, to_x_far)
    for peer in peers:
        pl.semaphore_signal(barrier, inc=1, device_id=peer, device_id_type=MESH)
    pl.semaphore_wait(barrier, len(peers))

    starts = []
    for _, _, _, tiles in CHUNKS:
        starts.append(starts[-1] + last if starts else 0)
        last = tiles * TILE

    def cols(k):
        return pl.ds(starts[k], CHUNKS[k][3] * TILE)

    def over_cols(k, work):
        start, tiles = starts[k], CHUNKS[k][3]
        step = 2 * TILE if tiles % 2 == 0 else TILE
        n = tiles * TILE // step
        if n == 1:
            work(pl.ds(start, step))
        else:
            def body(i, carry):
                work(pl.ds(pl.multiple_of(start + i * step, TILE), step))
                return carry

            lax.fori_loop(0, n, body, 0)

    def remote(k, slot, src, dst, device):
        return pltpu.make_async_remote_copy(
            src_ref=src, dst_ref=dst, send_sem=ssem.at[k, slot], recv_sem=rsem.at[k, slot],
            device_id=device, device_id_type=MESH,
        )

    def z_first(k):
        return CHUNKS[k][0]

    def early(k):
        return CHUNKS[k][1]

    def direct(k):
        return CHUNKS[k][2]

    def ring_slots(k):
        return (TO_UP, TO_DOWN, TO_FAR) if direct(k) else (RELAY_UP, RELAY_DOWN, DIRECT_UP, DIRECT_DOWN)

    def y_place(k, slot):
        return (4 + slot // 2, (slot % 2) * 32, 32) if z_first(k) else (slot, 0, 64)

    def y_in(k, slot):
        if direct(k):
            return got.at[4 + slot, :, cols(k)] if z_first(k) else got.at[2 * slot:2 * slot + 2, :, cols(k)]
        i, r, n = y_place(k, slot)
        return got.at[i, pl.ds(r, n), cols(k)]

    def y_copy(k, slot):
        if direct(k):
            block = (y_up, y_down, y_far)[slot]
            src = got.at[block, :, cols(k)] if z_first(k) else g_ref.at[block, :, :, cols(k)]
            return remote(k, slot, src, y_in(k, slot), (to_y_up, to_y_down, to_y_far)[slot])

        def part(block, half):
            if z_first(k):
                return got.at[block, pl.ds(half * 32, 32), cols(k)]
            return g_ref.at[block, half, :, cols(k)]

        src = {
            RELAY_UP: lambda: part(y_far, 0),
            RELAY_DOWN: lambda: part(y_far, 1),
            DIRECT_UP: lambda: part(y_up, 1),
            DIRECT_DOWN: lambda: part(y_down, 0),
            SECOND_UP: lambda: y_in(k, RELAY_UP),
            SECOND_DOWN: lambda: y_in(k, RELAY_DOWN),
        }[slot]()
        return remote(k, slot, src, y_in(k, slot), to_y_up if slot % 2 == 0 else to_y_down)

    def zl_copy(k):
        if z_first(k):
            return remote(k, Z_LO, g_ref.at[:, 1 - zl, :, cols(k)], got.at[0:4, :, cols(k)], to_zl)
        return remote(k, Z_LO, own.at[1 - zl, :, cols(k)], got.at[6, :, cols(k)], to_zl)

    def group_copies(k):
        if early(k):
            return (
                remote(k, Z_HI_CORE, dif.at[1 - core, 1 - zh, :, :, cols(k)], cr.at[1, :, :, cols(k)], to_both),
                remote(k, Z_HI, dif.at[core, 1 - zh, :, :, cols(k)], hr.at[:, :, cols(k)], to_zh),
                remote(k, CORE, dif.at[1 - core, zh, :, :, cols(k)], cr.at[0, :, :, cols(k)], to_core),
            )
        return (remote(k, CORE, dif.at[1 - core, :, :, :, cols(k)], cr.at[:, :, :, cols(k)], to_core),)

    def x_part(k, block, half):
        if early(k):
            return wgt.at[block, 0, :, pl.ds(half * 8, 8), cols(k)]
        return wgt.at[block, half, :, :, cols(k)]

    def x_in(k, slot):
        if direct(k):
            return xr.at[2 * slot, :, :, cols(k)] if early(k) else xr.at[2 * slot:2 * slot + 2, :, :, cols(k)]
        return xr.at[slot, :, pl.ds(0, 8 if early(k) else 16), cols(k)]

    def x_copy(k, slot):
        if direct(k):
            block = (x_up, x_down, x_far)[slot]
            src = wgt.at[block, 0, :, :, cols(k)] if early(k) else wgt.at[block, :, :, :, cols(k)]
            return remote(k, X_RING + slot, src, x_in(k, slot), (to_x_up, to_x_down, to_x_far)[slot])

        src = {
            RELAY_UP: lambda: x_part(k, x_far, 0),
            RELAY_DOWN: lambda: x_part(k, x_far, 1),
            DIRECT_UP: lambda: x_part(k, x_up, 1),
            DIRECT_DOWN: lambda: x_part(k, x_down, 0),
            SECOND_UP: lambda: x_in(k, RELAY_UP),
            SECOND_DOWN: lambda: x_in(k, RELAY_DOWN),
        }[slot]()
        return remote(k, X_RING + slot, src, x_in(k, slot), to_x_up if slot % 2 == 0 else to_x_down)

    def zh_copy(k):
        return remote(k, Z_HI, wgt.at[x, 1 - zh, :, :, cols(k)], hr.at[:, :, cols(k)], to_zh)

    def arrived(k, slot, buf):
        remote(k, slot, buf, buf, to_core).wait_recv()

    def loads(k):
        c = cols(k)
        if z_first(k):
            pairs = [(g_ref.at[:, zl, :, c], own.at[:, :, c])]
        elif direct(k):
            pairs = [(g_ref.at[y, :, :, c], own.at[0:2, :, c])]
        else:
            pairs = [
                (g_ref.at[y_up, 0, :, c], own.at[2, :, c]),
                (g_ref.at[y_down, 1, :, c], own.at[3, :, c]),
                (g_ref.at[y, :, :, c], own.at[0:2, :, c]),
            ]
        state = ((p_ref, np_ref), (m_ref, nm_ref), (v_ref, nv_ref))
        pairs += [(src.at[0, :, c], dst.at[0, :, c]) for src, dst in state]
        return [functools.partial(pltpu.make_async_copy, src, dst, lsem.at[k, i]) for i, (src, dst) in enumerate(pairs)]

    def begin(k):
        if z_first(k):
            zl_copy(k).start()
        else:
            for slot in ring_slots(k):
                y_copy(k, slot).start()
        for copy in loads(k):
            copy().start()

    def zsum(k):
        loads(k)[0]().wait()
        arrived(k, Z_LO, got.at[0:4, :, cols(k)])

        def add(block):
            def work(c):
                got[block, :, c] = got[block, :, c] + own[block, :, c]

            over_cols(k, work)

        if direct(k):
            for slot, block in ((TO_FAR, y_far), (TO_UP, y_up), (TO_DOWN, y_down)):
                add(block)
                y_copy(k, slot).start()
        else:
            add(y_far)
            y_copy(k, RELAY_UP).start()
            y_copy(k, RELAY_DOWN).start()
            add(y_up)
            y_copy(k, DIRECT_UP).start()
            add(y_down)
            y_copy(k, DIRECT_DOWN).start()
        add(y)

    def yrelay(k):
        for slot, block, onward in ((RELAY_UP, y_up, SECOND_UP), (RELAY_DOWN, y_down, SECOND_DOWN)):
            if not z_first(k):
                loads(k)[slot]().wait()
            arrived(k, slot, y_in(k, slot))
            i, r, n = y_place(k, slot)

            def work(c):
                if z_first(k):
                    mine = got[block, pl.ds(slot * 32, 32), c]
                else:
                    mine = own[2 + slot, :, c]
                got[i, pl.ds(r, n), c] = got[i, pl.ds(r, n), c] + mine

            over_cols(k, work)
            y_copy(k, onward).start()

    def yfinal(k):
        loads(k)[0 if direct(k) else 2]().wait()
        if direct(k):
            for slot in range(3):
                arrived(k, slot, y_in(k, slot))
        for turn, half in enumerate((1 - zl, zl)):
            if not direct(k):
                for slot in (3 - half, 4 + half):
                    arrived(k, slot, got.at[slot, :, cols(k)])

            def work(c):
                if direct(k):
                    own[half, :, c] = own[half, :, c] + got[half, :, c] + got[2 + half, :, c] + got[4 + half, :, c]
                else:
                    own[half, :, c] = own[half, :, c] + got[3 - half, :, c] + got[4 + half, :, c]

            over_cols(k, work)
            if turn == 0:
                zl_copy(k).start()

    def adam(k):
        for copy in loads(k)[-3:]:
            copy().wait()
        if z_first(k):
            for slot in range(3) if direct(k) else (DIRECT_DOWN, SECOND_UP, DIRECT_UP, SECOND_DOWN):
                arrived(k, slot, y_in(k, slot))
        else:
            arrived(k, Z_LO, got.at[6, :, cols(k)])
        bias_one = 1.0 - 0.9**10
        bias_two = 1.0 - 0.999**10

        def work(c):
            for q in range(4):
                r = pl.ds(q * 16, 16)
                if z_first(k) and direct(k):
                    grad = got[y, r, c] + got[4, r, c] + got[5, r, c] + got[6, r, c]
                elif z_first(k):
                    grad = got[y, r, c]
                    for slot in ((DIRECT_DOWN, SECOND_UP) if q < 2 else (DIRECT_UP, SECOND_DOWN)):
                        i, first_row, _ = y_place(k, slot)
                        grad = grad + got[i, pl.ds(first_row + (q % 2) * 16, 16), c]
                else:
                    grad = own[zl, r, c] + got[6, r, c]
                params, first, second = np_ref[0, r, c], nm_ref[0, r, c], nv_ref[0, r, c]
                square = grad * grad
                new_first = 0.9 * first + 0.1 * grad
                new_second = 0.999 * second + 0.001 * square
                step = new_first / bias_one / (jnp.sqrt(new_second / bias_two) + 1e-08) + 0.1 * params
                dif[q % 2, q // 2, 0, :, c] = step
                dif[q % 2, q // 2, 1, :, c] = grad - first
                dif[q % 2, q // 2, 2, :, c] = square - second
                np_ref[0, r, c] = params - 0.001 * step
                nm_ref[0, r, c] = new_first
                nv_ref[0, r, c] = new_second

        over_cols(k, work)
        for copy in group_copies(k):
            copy.start()

    def weigh(k):
        if early(k):
            arrived(k, CORE, cr.at[0, :, :, cols(k)])
            arrived(k, Z_HI, hr.at[:, :, cols(k)])
            arrived(k, Z_HI_CORE, cr.at[1, :, :, cols(k)])
        else:
            arrived(k, CORE, cr.at[:, :, :, cols(k)])

        def work(c):
            if early(k):
                fields = (dif[core, zh, :, :, c], cr[0, :, :, c], hr[:, :, c], cr[1, :, :, c])
                for j in range(4):
                    total = gen_ref[j, rec] * fields[0]
                    for member, field in zip((rec_core, rec_zh, rec_both), fields[1:]):
                        total = total + gen_ref[j, member] * field
                    wgt[j, 0, :, :, c] = total
            else:
                for half in range(2):
                    mine, other = dif[core, half, :, :, c], cr[half, :, :, c]
                    for j in range(4):
                        wgt[j, half, :, :, c] = gen_ref[j, rec] * mine + gen_ref[j, rec_core] * other

        over_cols(k, work)
        for slot in ring_slots(k):
            x_copy(k, slot).start()

    def xrelay(k):
        for slot, block, onward in ((RELAY_UP, x_up, SECOND_UP), (RELAY_DOWN, x_down, SECOND_DOWN)):
            arrived(k, X_RING + slot, x_in(k, slot))

            def work(c):
                if early(k):
                    r = pl.ds(0, 8)
                    xr[slot, :, r, c] = xr[slot, :, r, c] + wgt[block, 0, :, pl.ds(slot * 8, 8), c]
                else:
                    xr[slot, :, :, c] = xr[slot, :, :, c] + wgt[block, slot, :, :, c]

            over_cols(k, work)
            x_copy(k, onward).start()

    def xfinal(k):
        if direct(k):
            for slot in range(3):
                arrived(k, X_RING + slot, x_in(k, slot))

            def total(half, c):
                return wgt[x, half, :, :, c] + xr[half, :, :, c] + xr[2 + half, :, :, c] + xr[4 + half, :, :, c]

            if early(k):
                def work(c):
                    par_ref[0, 0, :, :, c] = total(0, c)

                over_cols(k, work)
                return
            for turn, half in enumerate((1 - zh, zh)):
                def work(c):
                    wgt[x, half, :, :, c] = total(half, c)

                over_cols(k, work)
                if turn == 0:
                    zh_copy(k).start()
            return
        if early(k):
            for slot in (DIRECT_DOWN, SECOND_UP, DIRECT_UP, SECOND_DOWN):
                arrived(k, X_RING + slot, x_in(k, slot))

            def work(c):
                r = pl.ds(0, 8)
                for half in range(2):
                    h = pl.ds(half * 8, 8)
                    par_ref[0, 0, :, h, c] = wgt[x, 0, :, h, c] + xr[3 - half, :, r, c] + xr[4 + half, :, r, c]

            over_cols(k, work)
            return
        for turn, half in enumerate((1 - zh, zh)):
            for slot in (3 - half, 4 + half):
                arrived(k, X_RING + slot, xr.at[slot, :, :, cols(k)])

            def work(c):
                wgt[x, half, :, :, c] = wgt[x, half, :, :, c] + xr[3 - half, :, :, c] + xr[4 + half, :, :, c]

            over_cols(k, work)
            if turn == 0:
                zh_copy(k).start()

    def finish(k):
        arrived(k, Z_HI, hr.at[:, :, cols(k)])

        def work(c):
            par_ref[0, 0, :, :, c] = wgt[x, zh, :, :, c] + hr[:, :, c]

        over_cols(k, work)

    stages = {
        BEGIN: begin, ZSUM: zsum, YRELAY: yrelay, YFINAL: yfinal, ADAM: adam,
        WEIGH: weigh, XRELAY: xrelay, XFINAL: xfinal, FINISH: finish,
    }
    for stage, k in ORDER:
        stages[stage](k)

    for k in range(len(CHUNKS)):
        for slot in range(3 if direct(k) else 6):
            y_copy(k, slot).wait_send()
            x_copy(k, slot).wait_send()
        zl_copy(k).wait_send()
        for copy in group_copies(k):
            copy.wait_send()
        if not early(k):
            zh_copy(k).wait_send()


def copy_out(*refs):
    n = len(refs) // 2
    sems = refs[-1]
    copies = []
    for i in range(4):
        src, dst = refs[i], refs[4 + i]
        for part in range(4):
            if i < 3:
                where = (0, pl.ds(part * 16, 16))
            elif part < 3:
                where = (0, 0, part)
            else:
                continue
            copies.append(pltpu.make_async_copy(src.at[where], dst.at[where], sems.at[i, part]))
    for copy in copies:
        copy.start()
    for copy in copies:
        copy.wait()


def per_device(grad_parts, params, first_moment, second_moment, generator):
    width = params.shape[2]
    assert sum(tiles for _, _, _, tiles in CHUNKS) * TILE == width
    n = len(CHUNKS)
    any_spec = pl.BlockSpec(memory_space=pl.ANY)
    f32 = jnp.float32
    outs = (jax.ShapeDtypeStruct(params.shape, f32),) * 3 + (jax.ShapeDtypeStruct((1, 1, 3, 16, width), f32),)
    results = pl.pallas_call(
        kernel,
        out_shape=tuple(pltpu.VMEM(out.shape, out.dtype) for out in outs),
        in_specs=[any_spec] * 4 + [pl.BlockSpec(memory_space=pltpu.SMEM)],
        out_specs=(pl.BlockSpec(memory_space=pltpu.VMEM),) * 4,
        scratch_shapes=[
            pltpu.VMEM((4, 64, width), f32),
            pltpu.VMEM((7, 64, width), f32),
            pltpu.VMEM((2, 2, 3, 16, width), f32),
            pltpu.VMEM((2, 3, 16, width), f32),
            pltpu.VMEM((4, 2, 3, 16, width), f32),
            pltpu.VMEM((6, 3, 16, width), f32),
            pltpu.VMEM((3, 16, width), f32),
            pltpu.SemaphoreType.DMA((n, SLOTS)),
            pltpu.SemaphoreType.DMA((n, SLOTS)),
            pltpu.SemaphoreType.DMA((n, LOADS)),
        ],
        compiler_params=pltpu.CompilerParams(
            collective_id=0, has_side_effects=True, vmem_limit_bytes=50 << 20
        ),
        cost_estimate=pl.CostEstimate(
            flops=100_000_000, bytes_accessed=60_000_000, transcendentals=458_752
        ),
        name="adam_parity",
    )(grad_parts.reshape(4, 2, 64, width), params, first_moment, second_moment, generator)
    return pl.pallas_call(
        copy_out,
        out_shape=outs,
        in_specs=[any_spec] * 4,
        out_specs=(any_spec,) * 4,
        scratch_shapes=[pltpu.SemaphoreType.DMA((4, 4))],
        compiler_params=pltpu.CompilerParams(vmem_limit_bytes=1 << 20),
        cost_estimate=pl.CostEstimate(flops=0, bytes_accessed=13_800_000, transcendentals=0),
        name="copy_out",
    )(*results)


def solution(mesh):
    in_specs = (
        P("dp", "rec", None, None),
        P("rec", "dp", None),
        P("rec", "dp", None),
        P("rec", "dp", None),
        P(),
    )
    out_specs = (
        P("rec", "dp", None),
        P("rec", "dp", None),
        P("rec", "dp", None),
        P("dp", "rec", None, None, None),
    )
    return jax.shard_map(
        per_device, mesh=mesh, in_specs=in_specs, out_specs=out_specs, check_vma=False
    )
```

```python
import functools

import jax
import jax.numpy as jnp
from jax import lax
from jax.experimental import pallas as pl
from jax.experimental.pallas import tpu as pltpu
from jax.sharding import PartitionSpec as P

MESH = pl.DeviceIdType.MESH
TILE = 128

CHUNKS = (
    (0, 0, 0, 0, 8), (1, 0, 0, 0, 3), (0, 0, 0, 0, 6), (1, 0, 0, 0, 6), (0, 0, 0, 0, 6), (1, 1, 0, 0, 3), (0, 0, 0, 0, 5),
    (1, 0, 0, 0, 2), (0, 0, 0, 0, 6), (1, 1, 0, 0, 3), (0, 0, 0, 0, 3), (0, 1, 0, 0, 2), (1, 1, 0, 0, 1), (0, 1, 0, 1, 2),
)
BEGIN, ZSUM, YRELAY, YFINAL, ADAM, WEIGH, XRELAY, XFINAL, FINISH = range(9)
ORDER = (
    (BEGIN, 0), (BEGIN, 1), (BEGIN, 3), (ZSUM, 1), (YRELAY, 0), (YRELAY, 1),
    (BEGIN, 2), (YFINAL, 0), (YRELAY, 2), (BEGIN, 5), (ZSUM, 3), (ADAM, 1),
    (WEIGH, 1), (BEGIN, 4), (ADAM, 0), (YFINAL, 2), (BEGIN, 7), (XRELAY, 1),
    (BEGIN, 9), (WEIGH, 0), (YRELAY, 3), (YRELAY, 4), (XRELAY, 0), (ZSUM, 5),
    (BEGIN, 6), (ADAM, 2), (WEIGH, 2), (ADAM, 3), (WEIGH, 3), (YRELAY, 5),
    (YFINAL, 4), (BEGIN, 12), (XRELAY, 2), (YRELAY, 6), (XFINAL, 1), (XRELAY, 3),
    (BEGIN, 8), (ADAM, 4), (ADAM, 5), (YFINAL, 6), (WEIGH, 4), (XFINAL, 0),
    (YRELAY, 8), (XFINAL, 2), (WEIGH, 5), (ZSUM, 9), (BEGIN, 10), (XRELAY, 4),
    (ADAM, 6), (ZSUM, 12), (WEIGH, 6), (YFINAL, 8), (XFINAL, 3), (YRELAY, 9),
    (XRELAY, 5), (YRELAY, 10), (XFINAL, 4), (XRELAY, 6), (BEGIN, 11), (ADAM, 8),
    (BEGIN, 13), (WEIGH, 8), (YFINAL, 10), (YRELAY, 11), (ADAM, 9), (ZSUM, 7),
    (ADAM, 10), (YRELAY, 13), (XRELAY, 8), (XFINAL, 6), (FINISH, 4), (YRELAY, 12),
    (YFINAL, 11), (YRELAY, 7), (WEIGH, 10), (YFINAL, 13), (ADAM, 12), (WEIGH, 9),
    (ADAM, 7), (ADAM, 11), (WEIGH, 7), (ADAM, 13), (FINISH, 6), (FINISH, 1),
    (XFINAL, 8), (XRELAY, 10), (WEIGH, 12), (XRELAY, 7), (XRELAY, 9), (WEIGH, 11),
    (XFINAL, 10), (WEIGH, 13), (XFINAL, 5), (FINISH, 3), (FINISH, 0), (XRELAY, 12),
    (XFINAL, 7), (XFINAL, 9), (XRELAY, 11), (XFINAL, 12), (FINISH, 8), (FINISH, 2),
    (FINISH, 10), (FINISH, 7), (XFINAL, 13), (XFINAL, 11),
)

RELAY_UP, RELAY_DOWN, DIRECT_UP, DIRECT_DOWN, SECOND_UP, SECOND_DOWN = range(6)
TO_UP, TO_DOWN, TO_FAR = range(3)
Z_LO, CORE, X_RING, Z_HI, Z_HI_CORE = 6, 7, 8, 14, 15
SLOTS = 16
LOADS = 6


def kernel(
    g_ref, p_ref, m_ref, v_ref, gen_ref,
    np_ref, nm_ref, nv_ref, par_ref,
    own, got, dif, cr, wgt, xr, hr,
    ssem, rsem, lsem,
):
    dp = lax.axis_index("dp")
    rec = lax.axis_index("rec")
    y, zl = dp // 2, dp % 2
    x, zh, core = rec // 4, (rec // 2) % 2, rec % 2
    y_up, y_down, y_far = (y + 1) % 4, (y + 3) % 4, (y + 2) % 4
    x_up, x_down, x_far = (x + 1) % 4, (x + 3) % 4, (x + 2) % 4
    to_y_up = (y_up * 2 + zl, rec)
    to_y_down = (y_down * 2 + zl, rec)
    to_y_far = (y_far * 2 + zl, rec)
    to_zl = (y * 2 + 1 - zl, rec)
    rec_core = x * 4 + zh * 2 + 1 - core
    rec_zh = x * 4 + (1 - zh) * 2 + core
    rec_both = x * 4 + (1 - zh) * 2 + 1 - core
    to_core, to_zh, to_both = (dp, rec_core), (dp, rec_zh), (dp, rec_both)
    to_x_up = (dp, x_up * 4 + zh * 2 + core)
    to_x_down = (dp, x_down * 4 + zh * 2 + core)

    to_x_far = (dp, x_far * 4 + zh * 2 + core)

    barrier = pltpu.get_barrier_semaphore()
    peers = (to_y_up, to_y_down, to_y_far, to_zl, to_core, to_zh, to_both, to_x_up, to_x_down, to_x_far)
    for peer in peers:
        pl.semaphore_signal(barrier, inc=1, device_id=peer, device_id_type=MESH)
    pl.semaphore_wait(barrier, len(peers))

    starts = []
    for _, _, _, _, tiles in CHUNKS:
        starts.append(starts[-1] + last if starts else 0)
        last = tiles * TILE

    def cols(k):
        return pl.ds(starts[k], CHUNKS[k][4] * TILE)

    def over_cols(k, work):
        start, tiles = starts[k], CHUNKS[k][4]
        step = 2 * TILE if tiles % 2 == 0 else TILE
        n = tiles * TILE // step
        if n == 1:
            work(pl.ds(start, step))
        else:
            def body(i, carry):
                work(pl.ds(pl.multiple_of(start + i * step, TILE), step))
                return carry

            lax.fori_loop(0, n, body, 0)

    def remote(k, slot, src, dst, device):
        return pltpu.make_async_remote_copy(
            src_ref=src, dst_ref=dst, send_sem=ssem.at[k, slot], recv_sem=rsem.at[k, slot],
            device_id=device, device_id_type=MESH,
        )

    def z_first(k):
        return CHUNKS[k][0]

    def early(k):
        return CHUNKS[k][1]

    def y_direct(k):
        return CHUNKS[k][2]

    def x_direct(k):
        return CHUNKS[k][3]

    def first_slots(direct):
        return (TO_UP, TO_DOWN, TO_FAR) if direct else (RELAY_UP, RELAY_DOWN, DIRECT_UP, DIRECT_DOWN)

    def y_place(k, slot):
        return (4 + slot // 2, (slot % 2) * 32, 32) if z_first(k) else (slot, 0, 64)

    def y_in(k, slot):
        if y_direct(k):
            return got.at[4 + slot, :, cols(k)] if z_first(k) else got.at[2 * slot:2 * slot + 2, :, cols(k)]
        i, r, n = y_place(k, slot)
        return got.at[i, pl.ds(r, n), cols(k)]

    def y_copy(k, slot):
        if y_direct(k):
            block = (y_up, y_down, y_far)[slot]
            src = got.at[block, :, cols(k)] if z_first(k) else g_ref.at[block, :, :, cols(k)]
            return remote(k, slot, src, y_in(k, slot), (to_y_up, to_y_down, to_y_far)[slot])

        def part(block, half):
            if z_first(k):
                return got.at[block, pl.ds(half * 32, 32), cols(k)]
            return g_ref.at[block, half, :, cols(k)]

        src = {
            RELAY_UP: lambda: part(y_far, 0),
            RELAY_DOWN: lambda: part(y_far, 1),
            DIRECT_UP: lambda: part(y_up, 1),
            DIRECT_DOWN: lambda: part(y_down, 0),
            SECOND_UP: lambda: y_in(k, RELAY_UP),
            SECOND_DOWN: lambda: y_in(k, RELAY_DOWN),
        }[slot]()
        return remote(k, slot, src, y_in(k, slot), to_y_up if slot % 2 == 0 else to_y_down)

    def zl_copy(k):
        if z_first(k):
            return remote(k, Z_LO, g_ref.at[:, 1 - zl, :, cols(k)], got.at[0:4, :, cols(k)], to_zl)
        return remote(k, Z_LO, own.at[1 - zl, :, cols(k)], got.at[6, :, cols(k)], to_zl)

    def group_copies(k):
        if early(k):
            return (
                remote(k, Z_HI_CORE, dif.at[1 - core, 1 - zh, :, :, cols(k)], cr.at[1, :, :, cols(k)], to_both),
                remote(k, Z_HI, dif.at[core, 1 - zh, :, :, cols(k)], hr.at[:, :, cols(k)], to_zh),
                remote(k, CORE, dif.at[1 - core, zh, :, :, cols(k)], cr.at[0, :, :, cols(k)], to_core),
            )
        return (remote(k, CORE, dif.at[1 - core, :, :, :, cols(k)], cr.at[:, :, :, cols(k)], to_core),)

    def x_part(k, block, half):
        if early(k):
            return wgt.at[block, 0, :, pl.ds(half * 8, 8), cols(k)]
        return wgt.at[block, half, :, :, cols(k)]

    def x_in(k, slot):
        if x_direct(k):
            return xr.at[2 * slot, :, :, cols(k)] if early(k) else xr.at[2 * slot:2 * slot + 2, :, :, cols(k)]
        return xr.at[slot, :, pl.ds(0, 8 if early(k) else 16), cols(k)]

    def x_copy(k, slot):
        if x_direct(k):
            block = (x_up, x_down, x_far)[slot]
            src = wgt.at[block, 0, :, :, cols(k)] if early(k) else wgt.at[block, :, :, :, cols(k)]
            return remote(k, X_RING + slot, src, x_in(k, slot), (to_x_up, to_x_down, to_x_far)[slot])

        src = {
            RELAY_UP: lambda: x_part(k, x_far, 0),
            RELAY_DOWN: lambda: x_part(k, x_far, 1),
            DIRECT_UP: lambda: x_part(k, x_up, 1),
            DIRECT_DOWN: lambda: x_part(k, x_down, 0),
            SECOND_UP: lambda: x_in(k, RELAY_UP),
            SECOND_DOWN: lambda: x_in(k, RELAY_DOWN),
        }[slot]()
        return remote(k, X_RING + slot, src, x_in(k, slot), to_x_up if slot % 2 == 0 else to_x_down)

    def zh_copy(k):
        return remote(k, Z_HI, wgt.at[x, 1 - zh, :, :, cols(k)], hr.at[:, :, cols(k)], to_zh)

    def arrived(k, slot, buf):
        remote(k, slot, buf, buf, to_core).wait_recv()

    def loads(k):
        c = cols(k)
        if z_first(k):
            pairs = [(g_ref.at[:, zl, :, c], own.at[:, :, c])]
        elif y_direct(k):
            pairs = [(g_ref.at[y, :, :, c], own.at[0:2, :, c])]
        else:
            pairs = [
                (g_ref.at[y_up, 0, :, c], own.at[2, :, c]),
                (g_ref.at[y_down, 1, :, c], own.at[3, :, c]),
                (g_ref.at[y, :, :, c], own.at[0:2, :, c]),
            ]
        state = ((p_ref, np_ref), (m_ref, nm_ref), (v_ref, nv_ref))
        pairs += [(src.at[0, :, c], dst.at[0, :, c]) for src, dst in state]
        return [functools.partial(pltpu.make_async_copy, src, dst, lsem.at[k, i]) for i, (src, dst) in enumerate(pairs)]

    def begin(k):
        if z_first(k):
            zl_copy(k).start()
        else:
            for slot in first_slots(y_direct(k)):
                y_copy(k, slot).start()
        for copy in loads(k):
            copy().start()

    def zsum(k):
        loads(k)[0]().wait()
        arrived(k, Z_LO, got.at[0:4, :, cols(k)])

        def add(block):
            def work(c):
                got[block, :, c] = got[block, :, c] + own[block, :, c]

            over_cols(k, work)

        if y_direct(k):
            for slot, block in ((TO_FAR, y_far), (TO_UP, y_up), (TO_DOWN, y_down)):
                add(block)
                y_copy(k, slot).start()
        else:
            add(y_far)
            y_copy(k, RELAY_UP).start()
            y_copy(k, RELAY_DOWN).start()
            add(y_up)
            y_copy(k, DIRECT_UP).start()
            add(y_down)
            y_copy(k, DIRECT_DOWN).start()
        add(y)

    def yrelay(k):
        for slot, block, onward in ((RELAY_UP, y_up, SECOND_UP), (RELAY_DOWN, y_down, SECOND_DOWN)):
            if not z_first(k):
                loads(k)[slot]().wait()
            arrived(k, slot, y_in(k, slot))
            i, r, n = y_place(k, slot)

            def work(c):
                if z_first(k):
                    mine = got[block, pl.ds(slot * 32, 32), c]
                else:
                    mine = own[2 + slot, :, c]
                got[i, pl.ds(r, n), c] = got[i, pl.ds(r, n), c] + mine

            over_cols(k, work)
            y_copy(k, onward).start()

    def yfinal(k):
        loads(k)[0 if y_direct(k) else 2]().wait()
        if y_direct(k):
            for slot in range(3):
                arrived(k, slot, y_in(k, slot))
        for turn, half in enumerate((1 - zl, zl)):
            if not y_direct(k):
                for slot in (3 - half, 4 + half):
                    arrived(k, slot, got.at[slot, :, cols(k)])

            def work(c):
                if y_direct(k):
                    own[half, :, c] = own[half, :, c] + got[half, :, c] + got[2 + half, :, c] + got[4 + half, :, c]
                else:
                    own[half, :, c] = own[half, :, c] + got[3 - half, :, c] + got[4 + half, :, c]

            over_cols(k, work)
            if turn == 0:
                zl_copy(k).start()

    def adam(k):
        for copy in loads(k)[-3:]:
            copy().wait()
        if z_first(k):
            for slot in range(3) if y_direct(k) else (DIRECT_DOWN, SECOND_UP, DIRECT_UP, SECOND_DOWN):
                arrived(k, slot, y_in(k, slot))
        else:
            arrived(k, Z_LO, got.at[6, :, cols(k)])
        bias_one = 1.0 - 0.9**10
        bias_two = 1.0 - 0.999**10

        def work(c):
            for q in range(4):
                r = pl.ds(q * 16, 16)
                if z_first(k) and y_direct(k):
                    grad = got[y, r, c] + got[4, r, c] + got[5, r, c] + got[6, r, c]
                elif z_first(k):
                    grad = got[y, r, c]
                    for slot in ((DIRECT_DOWN, SECOND_UP) if q < 2 else (DIRECT_UP, SECOND_DOWN)):
                        i, first_row, _ = y_place(k, slot)
                        grad = grad + got[i, pl.ds(first_row + (q % 2) * 16, 16), c]
                else:
                    grad = own[zl, r, c] + got[6, r, c]
                params, first, second = np_ref[0, r, c], nm_ref[0, r, c], nv_ref[0, r, c]
                square = grad * grad
                new_first = 0.9 * first + 0.1 * grad
                new_second = 0.999 * second + 0.001 * square
                step = new_first / bias_one / (jnp.sqrt(new_second / bias_two) + 1e-08) + 0.1 * params
                dif[q % 2, q // 2, 0, :, c] = step
                dif[q % 2, q // 2, 1, :, c] = grad - first
                dif[q % 2, q // 2, 2, :, c] = square - second
                np_ref[0, r, c] = params - 0.001 * step
                nm_ref[0, r, c] = new_first
                nv_ref[0, r, c] = new_second

        over_cols(k, work)
        for copy in group_copies(k):
            copy.start()

    def weigh(k):
        if early(k):
            arrived(k, CORE, cr.at[0, :, :, cols(k)])
            arrived(k, Z_HI, hr.at[:, :, cols(k)])
            arrived(k, Z_HI_CORE, cr.at[1, :, :, cols(k)])
        else:
            arrived(k, CORE, cr.at[:, :, :, cols(k)])

        def work(c):
            if early(k):
                fields = (dif[core, zh, :, :, c], cr[0, :, :, c], hr[:, :, c], cr[1, :, :, c])
                for j in range(4):
                    total = gen_ref[j, rec] * fields[0]
                    for member, field in zip((rec_core, rec_zh, rec_both), fields[1:]):
                        total = total + gen_ref[j, member] * field
                    wgt[j, 0, :, :, c] = total
            else:
                for half in range(2):
                    mine, other = dif[core, half, :, :, c], cr[half, :, :, c]
                    for j in range(4):
                        wgt[j, half, :, :, c] = gen_ref[j, rec] * mine + gen_ref[j, rec_core] * other

        over_cols(k, work)
        for slot in first_slots(x_direct(k)):
            x_copy(k, slot).start()

    def xrelay(k):
        for slot, block, onward in ((RELAY_UP, x_up, SECOND_UP), (RELAY_DOWN, x_down, SECOND_DOWN)):
            arrived(k, X_RING + slot, x_in(k, slot))

            def work(c):
                if early(k):
                    r = pl.ds(0, 8)
                    xr[slot, :, r, c] = xr[slot, :, r, c] + wgt[block, 0, :, pl.ds(slot * 8, 8), c]
                else:
                    xr[slot, :, :, c] = xr[slot, :, :, c] + wgt[block, slot, :, :, c]

            over_cols(k, work)
            x_copy(k, onward).start()

    def xfinal(k):
        if x_direct(k):
            for slot in range(3):
                arrived(k, X_RING + slot, x_in(k, slot))

            def total(half, c):
                return wgt[x, half, :, :, c] + xr[half, :, :, c] + xr[2 + half, :, :, c] + xr[4 + half, :, :, c]

            if early(k):
                def work(c):
                    par_ref[0, 0, :, :, c] = total(0, c)

                over_cols(k, work)
                return
            for turn, half in enumerate((1 - zh, zh)):
                def work(c):
                    wgt[x, half, :, :, c] = total(half, c)

                over_cols(k, work)
                if turn == 0:
                    zh_copy(k).start()
            return
        if early(k):
            for slot in (DIRECT_DOWN, SECOND_UP, DIRECT_UP, SECOND_DOWN):
                arrived(k, X_RING + slot, x_in(k, slot))

            def work(c):
                r = pl.ds(0, 8)
                for half in range(2):
                    h = pl.ds(half * 8, 8)
                    par_ref[0, 0, :, h, c] = wgt[x, 0, :, h, c] + xr[3 - half, :, r, c] + xr[4 + half, :, r, c]

            over_cols(k, work)
            return
        for turn, half in enumerate((1 - zh, zh)):
            for slot in (3 - half, 4 + half):
                arrived(k, X_RING + slot, xr.at[slot, :, :, cols(k)])

            def work(c):
                wgt[x, half, :, :, c] = wgt[x, half, :, :, c] + xr[3 - half, :, :, c] + xr[4 + half, :, :, c]

            over_cols(k, work)
            if turn == 0:
                zh_copy(k).start()

    def finish(k):
        arrived(k, Z_HI, hr.at[:, :, cols(k)])

        def work(c):
            par_ref[0, 0, :, :, c] = wgt[x, zh, :, :, c] + hr[:, :, c]

        over_cols(k, work)

    stages = {
        BEGIN: begin, ZSUM: zsum, YRELAY: yrelay, YFINAL: yfinal, ADAM: adam,
        WEIGH: weigh, XRELAY: xrelay, XFINAL: xfinal, FINISH: finish,
    }
    for stage, k in ORDER:
        stages[stage](k)

    for k in range(len(CHUNKS)):
        for slot in range(3 if y_direct(k) else 6):
            y_copy(k, slot).wait_send()
        for slot in range(3 if x_direct(k) else 6):
            x_copy(k, slot).wait_send()
        zl_copy(k).wait_send()
        for copy in group_copies(k):
            copy.wait_send()
        if not early(k):
            zh_copy(k).wait_send()


def copy_out(*refs):
    n = len(refs) // 2
    sems = refs[-1]
    copies = []
    for i in range(4):
        src, dst = refs[i], refs[4 + i]
        for part in range(4):
            if i < 3:
                where = (0, pl.ds(part * 16, 16))
            elif part < 3:
                where = (0, 0, part)
            else:
                continue
            copies.append(pltpu.make_async_copy(src.at[where], dst.at[where], sems.at[i, part]))
    for copy in copies:
        copy.start()
    for copy in copies:
        copy.wait()


def per_device(grad_parts, params, first_moment, second_moment, generator):
    width = params.shape[2]
    assert sum(tiles for _, _, _, _, tiles in CHUNKS) * TILE == width
    n = len(CHUNKS)
    any_spec = pl.BlockSpec(memory_space=pl.ANY)
    f32 = jnp.float32
    outs = (jax.ShapeDtypeStruct(params.shape, f32),) * 3 + (jax.ShapeDtypeStruct((1, 1, 3, 16, width), f32),)
    results = pl.pallas_call(
        kernel,
        out_shape=tuple(pltpu.VMEM(out.shape, out.dtype) for out in outs),
        in_specs=[any_spec] * 4 + [pl.BlockSpec(memory_space=pltpu.SMEM)],
        out_specs=(pl.BlockSpec(memory_space=pltpu.VMEM),) * 4,
        scratch_shapes=[
            pltpu.VMEM((4, 64, width), f32),
            pltpu.VMEM((7, 64, width), f32),
            pltpu.VMEM((2, 2, 3, 16, width), f32),
            pltpu.VMEM((2, 3, 16, width), f32),
            pltpu.VMEM((4, 2, 3, 16, width), f32),
            pltpu.VMEM((6, 3, 16, width), f32),
            pltpu.VMEM((3, 16, width), f32),
            pltpu.SemaphoreType.DMA((n, SLOTS)),
            pltpu.SemaphoreType.DMA((n, SLOTS)),
            pltpu.SemaphoreType.DMA((n, LOADS)),
        ],
        compiler_params=pltpu.CompilerParams(
            collective_id=0, has_side_effects=True, vmem_limit_bytes=50 << 20
        ),
        cost_estimate=pl.CostEstimate(
            flops=100_000_000, bytes_accessed=60_000_000, transcendentals=458_752
        ),
        name="adam_parity",
    )(grad_parts.reshape(4, 2, 64, width), params, first_moment, second_moment, generator)
    return pl.pallas_call(
        copy_out,
        out_shape=outs,
        in_specs=[any_spec] * 4,
        out_specs=(any_spec,) * 4,
        scratch_shapes=[pltpu.SemaphoreType.DMA((4, 4))],
        compiler_params=pltpu.CompilerParams(vmem_limit_bytes=1 << 20),
        cost_estimate=pl.CostEstimate(flops=0, bytes_accessed=13_800_000, transcendentals=0),
        name="copy_out",
    )(*results)


def solution(mesh):
    in_specs = (
        P("dp", "rec", None, None),
        P("rec", "dp", None),
        P("rec", "dp", None),
        P("rec", "dp", None),
        P(),
    )
    out_specs = (
        P("rec", "dp", None),
        P("rec", "dp", None),
        P("rec", "dp", None),
        P("dp", "rec", None, None, None),
    )
    return jax.shard_map(
        per_device, mesh=mesh, in_specs=in_specs, out_specs=out_specs, check_vma=False
    )
```

```python
import functools

import jax
import jax.numpy as jnp
from jax import lax
from jax.experimental import pallas as pl
from jax.experimental.pallas import tpu as pltpu
from jax.sharding import PartitionSpec as P

MESH = pl.DeviceIdType.MESH
TILE = 128

CHUNKS = (
    (0, 0, 0, 0, 8), (1, 0, 0, 0, 3), (0, 0, 0, 0, 6), (1, 0, 0, 0, 6), (0, 0, 0, 0, 6), (1, 1, 0, 0, 3), (0, 0, 0, 0, 5),
    (1, 0, 0, 0, 2), (0, 0, 0, 0, 6), (1, 1, 0, 0, 3), (0, 0, 0, 0, 3), (0, 1, 0, 0, 2), (1, 1, 0, 0, 1), (0, 1, 0, 1, 2),
)
BEGIN, ZSUM, YRELAY, YFINAL, ADAM, WEIGH, XRELAY, XFINAL, FINISH = range(9)
ORDER = (
    (BEGIN, 0), (BEGIN, 1), (BEGIN, 3), (ZSUM, 1), (YRELAY, 0), (YRELAY, 1),
    (BEGIN, 2), (YFINAL, 0), (YRELAY, 2), (BEGIN, 5), (ZSUM, 3), (ADAM, 1),
    (WEIGH, 1), (BEGIN, 4), (ADAM, 0), (YFINAL, 2), (BEGIN, 7), (XRELAY, 1),
    (BEGIN, 9), (WEIGH, 0), (YRELAY, 3), (YRELAY, 4), (XRELAY, 0), (ZSUM, 5),
    (BEGIN, 6), (ADAM, 2), (WEIGH, 2), (ADAM, 3), (WEIGH, 3), (YRELAY, 5),
    (YFINAL, 4), (BEGIN, 12), (XRELAY, 2), (YRELAY, 6), (XFINAL, 1), (XRELAY, 3),
    (BEGIN, 8), (ADAM, 4), (ADAM, 5), (YFINAL, 6), (WEIGH, 4), (XFINAL, 0),
    (YRELAY, 8), (XFINAL, 2), (WEIGH, 5), (ZSUM, 9), (BEGIN, 10), (XRELAY, 4),
    (ADAM, 6), (ZSUM, 12), (WEIGH, 6), (YFINAL, 8), (XFINAL, 3), (YRELAY, 9),
    (XRELAY, 5), (YRELAY, 10), (XFINAL, 4), (XRELAY, 6), (BEGIN, 11), (ADAM, 8),
    (BEGIN, 13), (WEIGH, 8), (YFINAL, 10), (YRELAY, 11), (ADAM, 9), (ZSUM, 7),
    (ADAM, 10), (YRELAY, 13), (XRELAY, 8), (XFINAL, 6), (FINISH, 4), (YRELAY, 12),
    (YFINAL, 11), (YRELAY, 7), (WEIGH, 10), (YFINAL, 13), (ADAM, 12), (WEIGH, 9),
    (ADAM, 7), (ADAM, 11), (WEIGH, 7), (ADAM, 13), (FINISH, 6), (FINISH, 1),
    (XFINAL, 8), (XRELAY, 10), (WEIGH, 12), (XRELAY, 7), (XRELAY, 9), (WEIGH, 11),
    (XFINAL, 10), (WEIGH, 13), (XFINAL, 5), (FINISH, 3), (FINISH, 0), (XRELAY, 12),
    (XFINAL, 7), (XFINAL, 9), (XRELAY, 11), (XFINAL, 12), (FINISH, 8), (FINISH, 2),
    (FINISH, 10), (FINISH, 7), (XFINAL, 13), (XFINAL, 11),
)

RELAY_UP, RELAY_DOWN, DIRECT_UP, DIRECT_DOWN, SECOND_UP, SECOND_DOWN = range(6)
TO_UP, TO_DOWN, TO_FAR = range(3)
Z_LO, CORE, X_RING, Z_HI, Z_HI_CORE = 6, 7, 8, 14, 15
SLOTS = 16
LOADS = 6
SETTLE = 16


def kernel(
    g_ref, p_ref, m_ref, v_ref, gen_ref,
    np_ref, nm_ref, nv_ref, par_ref,
    own, got, dif, cr, wgt, xr, hr,
    ssem, rsem, lsem,
):
    dp = lax.axis_index("dp")
    rec = lax.axis_index("rec")
    y, zl = dp // 2, dp % 2
    x, zh, core = rec // 4, (rec // 2) % 2, rec % 2
    y_up, y_down, y_far = (y + 1) % 4, (y + 3) % 4, (y + 2) % 4
    x_up, x_down, x_far = (x + 1) % 4, (x + 3) % 4, (x + 2) % 4
    to_y_up = (y_up * 2 + zl, rec)
    to_y_down = (y_down * 2 + zl, rec)
    to_y_far = (y_far * 2 + zl, rec)
    to_zl = (y * 2 + 1 - zl, rec)
    rec_core = x * 4 + zh * 2 + 1 - core
    rec_zh = x * 4 + (1 - zh) * 2 + core
    rec_both = x * 4 + (1 - zh) * 2 + 1 - core
    to_core, to_zh, to_both = (dp, rec_core), (dp, rec_zh), (dp, rec_both)
    to_x_up = (dp, x_up * 4 + zh * 2 + core)
    to_x_down = (dp, x_down * 4 + zh * 2 + core)

    to_x_far = (dp, x_far * 4 + zh * 2 + core)

    def z_first(k):
        return CHUNKS[k][0]

    def early(k):
        return CHUNKS[k][1]

    def y_direct(k):
        return CHUNKS[k][2]

    def x_direct(k):
        return CHUNKS[k][3]

    barrier = pltpu.get_barrier_semaphore()
    peers = [to_y_up, to_y_down, to_zl, to_core, to_zh, to_x_up, to_x_down]
    peers += [to_both] if any(early(k) for k in range(len(CHUNKS))) else []
    peers += [to_y_far] if any(y_direct(k) for k in range(len(CHUNKS))) else []
    peers += [to_x_far] if any(x_direct(k) for k in range(len(CHUNKS))) else []
    for peer in peers:
        pl.semaphore_signal(barrier, inc=1, device_id=peer, device_id_type=MESH)
    pl.semaphore_wait(barrier, len(peers))

    starts = []
    for _, _, _, _, tiles in CHUNKS:
        starts.append(starts[-1] + last if starts else 0)
        last = tiles * TILE

    def cols(k):
        return pl.ds(starts[k], CHUNKS[k][4] * TILE)

    def over_cols(k, work):
        start, tiles = starts[k], CHUNKS[k][4]
        step = 2 * TILE if tiles % 2 == 0 else TILE
        n = tiles * TILE // step
        if n == 1:
            work(pl.ds(start, step))
        else:
            def body(i, carry):
                work(pl.ds(pl.multiple_of(start + i * step, TILE), step))
                return carry

            lax.fori_loop(0, n, body, 0)

    def remote(k, slot, src, dst, device):
        return pltpu.make_async_remote_copy(
            src_ref=src, dst_ref=dst, send_sem=ssem.at[k, slot], recv_sem=rsem.at[k, slot],
            device_id=device, device_id_type=MESH,
        )

    def first_slots(direct):
        return (TO_UP, TO_DOWN, TO_FAR) if direct else (RELAY_UP, RELAY_DOWN, DIRECT_UP, DIRECT_DOWN)

    def y_place(k, slot):
        return (4 + slot // 2, (slot % 2) * 32, 32) if z_first(k) else (slot, 0, 64)

    def y_in(k, slot):
        if y_direct(k):
            return got.at[4 + slot, :, cols(k)] if z_first(k) else got.at[2 * slot:2 * slot + 2, :, cols(k)]
        i, r, n = y_place(k, slot)
        return got.at[i, pl.ds(r, n), cols(k)]

    def y_copy(k, slot):
        if y_direct(k):
            block = (y_up, y_down, y_far)[slot]
            src = got.at[block, :, cols(k)] if z_first(k) else g_ref.at[block, :, :, cols(k)]
            return remote(k, slot, src, y_in(k, slot), (to_y_up, to_y_down, to_y_far)[slot])

        def part(block, half):
            if z_first(k):
                return got.at[block, pl.ds(half * 32, 32), cols(k)]
            return g_ref.at[block, half, :, cols(k)]

        src = {
            RELAY_UP: lambda: part(y_far, 0),
            RELAY_DOWN: lambda: part(y_far, 1),
            DIRECT_UP: lambda: part(y_up, 1),
            DIRECT_DOWN: lambda: part(y_down, 0),
            SECOND_UP: lambda: y_in(k, RELAY_UP),
            SECOND_DOWN: lambda: y_in(k, RELAY_DOWN),
        }[slot]()
        return remote(k, slot, src, y_in(k, slot), to_y_up if slot % 2 == 0 else to_y_down)

    def zl_copy(k):
        if z_first(k):
            return remote(k, Z_LO, g_ref.at[:, 1 - zl, :, cols(k)], got.at[0:4, :, cols(k)], to_zl)
        return remote(k, Z_LO, own.at[1 - zl, :, cols(k)], got.at[6, :, cols(k)], to_zl)

    def group_copies(k):
        if early(k):
            return (
                remote(k, Z_HI_CORE, dif.at[1 - core, 1 - zh, :, :, cols(k)], cr.at[1, :, :, cols(k)], to_both),
                remote(k, Z_HI, dif.at[core, 1 - zh, :, :, cols(k)], hr.at[:, :, cols(k)], to_zh),
                remote(k, CORE, dif.at[1 - core, zh, :, :, cols(k)], cr.at[0, :, :, cols(k)], to_core),
            )
        return (remote(k, CORE, dif.at[1 - core, :, :, :, cols(k)], cr.at[:, :, :, cols(k)], to_core),)

    def x_part(k, block, half):
        if early(k):
            return wgt.at[block, 0, :, pl.ds(half * 8, 8), cols(k)]
        return wgt.at[block, half, :, :, cols(k)]

    def x_in(k, slot):
        if x_direct(k):
            return xr.at[2 * slot, :, :, cols(k)] if early(k) else xr.at[2 * slot:2 * slot + 2, :, :, cols(k)]
        return xr.at[slot, :, pl.ds(0, 8 if early(k) else 16), cols(k)]

    def x_copy(k, slot):
        if x_direct(k):
            block = (x_up, x_down, x_far)[slot]
            src = wgt.at[block, 0, :, :, cols(k)] if early(k) else wgt.at[block, :, :, :, cols(k)]
            return remote(k, X_RING + slot, src, x_in(k, slot), (to_x_up, to_x_down, to_x_far)[slot])

        src = {
            RELAY_UP: lambda: x_part(k, x_far, 0),
            RELAY_DOWN: lambda: x_part(k, x_far, 1),
            DIRECT_UP: lambda: x_part(k, x_up, 1),
            DIRECT_DOWN: lambda: x_part(k, x_down, 0),
            SECOND_UP: lambda: x_in(k, RELAY_UP),
            SECOND_DOWN: lambda: x_in(k, RELAY_DOWN),
        }[slot]()
        return remote(k, X_RING + slot, src, x_in(k, slot), to_x_up if slot % 2 == 0 else to_x_down)

    def zh_copy(k):
        return remote(k, Z_HI, wgt.at[x, 1 - zh, :, :, cols(k)], hr.at[:, :, cols(k)], to_zh)

    def arrived(k, slot, buf):
        remote(k, slot, buf, buf, to_core).wait_recv()

    def loads(k):
        c = cols(k)
        if z_first(k):
            pairs = [(g_ref.at[:, zl, :, c], own.at[:, :, c])]
        elif y_direct(k):
            pairs = [(g_ref.at[y, :, :, c], own.at[0:2, :, c])]
        else:
            pairs = [
                (g_ref.at[y_up, 0, :, c], own.at[2, :, c]),
                (g_ref.at[y_down, 1, :, c], own.at[3, :, c]),
                (g_ref.at[y, :, :, c], own.at[0:2, :, c]),
            ]
        state = ((p_ref, np_ref), (m_ref, nm_ref), (v_ref, nv_ref))
        pairs += [(src.at[0, :, c], dst.at[0, :, c]) for src, dst in state]
        return [functools.partial(pltpu.make_async_copy, src, dst, lsem.at[k, i]) for i, (src, dst) in enumerate(pairs)]

    def begin(k):
        if z_first(k):
            zl_copy(k).start()
        else:
            for slot in first_slots(y_direct(k)):
                y_copy(k, slot).start()
        for copy in loads(k):
            copy().start()

    def zsum(k):
        loads(k)[0]().wait()
        arrived(k, Z_LO, got.at[0:4, :, cols(k)])

        def add(block):
            def work(c):
                got[block, :, c] = got[block, :, c] + own[block, :, c]

            over_cols(k, work)

        if y_direct(k):
            for slot, block in ((TO_FAR, y_far), (TO_UP, y_up), (TO_DOWN, y_down)):
                add(block)
                y_copy(k, slot).start()
        else:
            add(y_far)
            y_copy(k, RELAY_UP).start()
            y_copy(k, RELAY_DOWN).start()
            add(y_up)
            y_copy(k, DIRECT_UP).start()
            add(y_down)
            y_copy(k, DIRECT_DOWN).start()
        add(y)

    def yrelay(k):
        for slot, block, onward in ((RELAY_UP, y_up, SECOND_UP), (RELAY_DOWN, y_down, SECOND_DOWN)):
            if not z_first(k):
                loads(k)[slot]().wait()
            arrived(k, slot, y_in(k, slot))
            i, r, n = y_place(k, slot)

            def work(c):
                if z_first(k):
                    mine = got[block, pl.ds(slot * 32, 32), c]
                else:
                    mine = own[2 + slot, :, c]
                got[i, pl.ds(r, n), c] = got[i, pl.ds(r, n), c] + mine

            over_cols(k, work)
            y_copy(k, onward).start()

    def yfinal(k):
        loads(k)[0 if y_direct(k) else 2]().wait()
        if y_direct(k):
            for slot in range(3):
                arrived(k, slot, y_in(k, slot))
        for turn, half in enumerate((1 - zl, zl)):
            if not y_direct(k):
                for slot in (3 - half, 4 + half):
                    arrived(k, slot, got.at[slot, :, cols(k)])

            def work(c):
                if y_direct(k):
                    own[half, :, c] = own[half, :, c] + got[half, :, c] + got[2 + half, :, c] + got[4 + half, :, c]
                else:
                    own[half, :, c] = own[half, :, c] + got[3 - half, :, c] + got[4 + half, :, c]

            over_cols(k, work)
            if turn == 0:
                zl_copy(k).start()

    def adam(k):
        for copy in loads(k)[-3:]:
            copy().wait()
        if z_first(k):
            for slot in range(3) if y_direct(k) else (DIRECT_DOWN, SECOND_UP, DIRECT_UP, SECOND_DOWN):
                arrived(k, slot, y_in(k, slot))
        else:
            arrived(k, Z_LO, got.at[6, :, cols(k)])
        bias_one = 1.0 - 0.9**10
        bias_two = 1.0 - 0.999**10

        def work(c):
            for q in range(4):
                r = pl.ds(q * 16, 16)
                if z_first(k) and y_direct(k):
                    grad = got[y, r, c] + got[4, r, c] + got[5, r, c] + got[6, r, c]
                elif z_first(k):
                    grad = got[y, r, c]
                    for slot in ((DIRECT_DOWN, SECOND_UP) if q < 2 else (DIRECT_UP, SECOND_DOWN)):
                        i, first_row, _ = y_place(k, slot)
                        grad = grad + got[i, pl.ds(first_row + (q % 2) * 16, 16), c]
                else:
                    grad = own[zl, r, c] + got[6, r, c]
                params, first, second = np_ref[0, r, c], nm_ref[0, r, c], nv_ref[0, r, c]
                square = grad * grad
                new_first = 0.9 * first + 0.1 * grad
                new_second = 0.999 * second + 0.001 * square
                step = new_first / bias_one / (jnp.sqrt(new_second / bias_two) + 1e-08) + 0.1 * params
                dif[q % 2, q // 2, 0, :, c] = step
                dif[q % 2, q // 2, 1, :, c] = grad - first
                dif[q % 2, q // 2, 2, :, c] = square - second
                np_ref[0, r, c] = params - 0.001 * step
                nm_ref[0, r, c] = new_first
                nv_ref[0, r, c] = new_second

        over_cols(k, work)
        for copy in group_copies(k):
            copy.start()

    def weigh(k):
        if early(k):
            arrived(k, CORE, cr.at[0, :, :, cols(k)])
            arrived(k, Z_HI, hr.at[:, :, cols(k)])
            arrived(k, Z_HI_CORE, cr.at[1, :, :, cols(k)])
        else:
            arrived(k, CORE, cr.at[:, :, :, cols(k)])

        def work(c):
            if early(k):
                fields = (dif[core, zh, :, :, c], cr[0, :, :, c], hr[:, :, c], cr[1, :, :, c])
                for j in range(4):
                    total = gen_ref[j, rec] * fields[0]
                    for member, field in zip((rec_core, rec_zh, rec_both), fields[1:]):
                        total = total + gen_ref[j, member] * field
                    wgt[j, 0, :, :, c] = total
            else:
                for half in range(2):
                    mine, other = dif[core, half, :, :, c], cr[half, :, :, c]
                    for j in range(4):
                        wgt[j, half, :, :, c] = gen_ref[j, rec] * mine + gen_ref[j, rec_core] * other

        over_cols(k, work)
        for slot in first_slots(x_direct(k)):
            x_copy(k, slot).start()

    def xrelay(k):
        for slot, block, onward in ((RELAY_UP, x_up, SECOND_UP), (RELAY_DOWN, x_down, SECOND_DOWN)):
            arrived(k, X_RING + slot, x_in(k, slot))

            def work(c):
                if early(k):
                    r = pl.ds(0, 8)
                    xr[slot, :, r, c] = xr[slot, :, r, c] + wgt[block, 0, :, pl.ds(slot * 8, 8), c]
                else:
                    xr[slot, :, :, c] = xr[slot, :, :, c] + wgt[block, slot, :, :, c]

            over_cols(k, work)
            x_copy(k, onward).start()

    def xfinal(k):
        if x_direct(k):
            for slot in range(3):
                arrived(k, X_RING + slot, x_in(k, slot))

            def total(half, c):
                return wgt[x, half, :, :, c] + xr[half, :, :, c] + xr[2 + half, :, :, c] + xr[4 + half, :, :, c]

            if early(k):
                def work(c):
                    par_ref[0, 0, :, :, c] = total(0, c)

                over_cols(k, work)
                return
            for turn, half in enumerate((1 - zh, zh)):
                def work(c):
                    wgt[x, half, :, :, c] = total(half, c)

                over_cols(k, work)
                if turn == 0:
                    zh_copy(k).start()
            return
        if early(k):
            for slot in (DIRECT_DOWN, SECOND_UP, DIRECT_UP, SECOND_DOWN):
                arrived(k, X_RING + slot, x_in(k, slot))

            def work(c):
                r = pl.ds(0, 8)
                for half in range(2):
                    h = pl.ds(half * 8, 8)
                    par_ref[0, 0, :, h, c] = wgt[x, 0, :, h, c] + xr[3 - half, :, r, c] + xr[4 + half, :, r, c]

            over_cols(k, work)
            return
        for turn, half in enumerate((1 - zh, zh)):
            for slot in (3 - half, 4 + half):
                arrived(k, X_RING + slot, xr.at[slot, :, :, cols(k)])

            def work(c):
                wgt[x, half, :, :, c] = wgt[x, half, :, :, c] + xr[3 - half, :, :, c] + xr[4 + half, :, :, c]

            over_cols(k, work)
            if turn == 0:
                zh_copy(k).start()

    def finish(k):
        arrived(k, Z_HI, hr.at[:, :, cols(k)])

        def work(c):
            par_ref[0, 0, :, :, c] = wgt[x, zh, :, :, c] + hr[:, :, c]

        over_cols(k, work)

    def gradient_sent(k):
        for slot in range(3 if y_direct(k) else 6):
            y_copy(k, slot).wait_send()
        zl_copy(k).wait_send()

    def parity_sent(k):
        for copy in group_copies(k):
            copy.wait_send()
        for slot in range(3 if x_direct(k) else 6):
            x_copy(k, slot).wait_send()
        if not early(k):
            zh_copy(k).wait_send()

    stages = {
        BEGIN: begin, ZSUM: zsum, YRELAY: yrelay, YFINAL: yfinal, ADAM: adam,
        WEIGH: weigh, XRELAY: xrelay, XFINAL: xfinal, FINISH: finish,
    }
    last = {k: at for at, (_, k) in enumerate(ORDER)}
    for at, (stage, k) in enumerate(ORDER):
        stages[stage](k)
        if stage == WEIGH:
            gradient_sent(k)
        for j in range(len(CHUNKS)):
            if last[j] + SETTLE == at:
                parity_sent(j)
    for j in range(len(CHUNKS)):
        if last[j] + SETTLE >= len(ORDER):
            parity_sent(j)


def copy_out(*refs):
    n = len(refs) // 2
    sems = refs[-1]
    copies = []
    for i in range(4):
        src, dst = refs[i], refs[4 + i]
        for part in range(4):
            if i < 3:
                where = (0, pl.ds(part * 16, 16))
            elif part < 3:
                where = (0, 0, part)
            else:
                continue
            copies.append(pltpu.make_async_copy(src.at[where], dst.at[where], sems.at[i, part]))
    for copy in copies:
        copy.start()
    for copy in copies:
        copy.wait()


def per_device(grad_parts, params, first_moment, second_moment, generator):
    width = params.shape[2]
    assert sum(tiles for _, _, _, _, tiles in CHUNKS) * TILE == width
    n = len(CHUNKS)
    any_spec = pl.BlockSpec(memory_space=pl.ANY)
    f32 = jnp.float32
    outs = (jax.ShapeDtypeStruct(params.shape, f32),) * 3 + (jax.ShapeDtypeStruct((1, 1, 3, 16, width), f32),)
    results = pl.pallas_call(
        kernel,
        out_shape=tuple(pltpu.VMEM(out.shape, out.dtype) for out in outs),
        in_specs=[any_spec] * 4 + [pl.BlockSpec(memory_space=pltpu.SMEM)],
        out_specs=(pl.BlockSpec(memory_space=pltpu.VMEM),) * 4,
        scratch_shapes=[
            pltpu.VMEM((4, 64, width), f32),
            pltpu.VMEM((7, 64, width), f32),
            pltpu.VMEM((2, 2, 3, 16, width), f32),
            pltpu.VMEM((2, 3, 16, width), f32),
            pltpu.VMEM((4, 2, 3, 16, width), f32),
            pltpu.VMEM((6, 3, 16, width), f32),
            pltpu.VMEM((3, 16, width), f32),
            pltpu.SemaphoreType.DMA((n, SLOTS)),
            pltpu.SemaphoreType.DMA((n, SLOTS)),
            pltpu.SemaphoreType.DMA((n, LOADS)),
        ],
        compiler_params=pltpu.CompilerParams(
            collective_id=0, has_side_effects=True, vmem_limit_bytes=50 << 20
        ),
        cost_estimate=pl.CostEstimate(
            flops=100_000_000, bytes_accessed=60_000_000, transcendentals=458_752
        ),
        name="adam_parity",
    )(grad_parts.reshape(4, 2, 64, width), params, first_moment, second_moment, generator)
    return pl.pallas_call(
        copy_out,
        out_shape=outs,
        in_specs=[any_spec] * 4,
        out_specs=(any_spec,) * 4,
        scratch_shapes=[pltpu.SemaphoreType.DMA((4, 4))],
        compiler_params=pltpu.CompilerParams(vmem_limit_bytes=1 << 20),
        cost_estimate=pl.CostEstimate(flops=0, bytes_accessed=13_800_000, transcendentals=0),
        name="copy_out",
    )(*results)


def solution(mesh):
    in_specs = (
        P("dp", "rec", None, None),
        P("rec", "dp", None),
        P("rec", "dp", None),
        P("rec", "dp", None),
        P(),
    )
    out_specs = (
        P("rec", "dp", None),
        P("rec", "dp", None),
        P("rec", "dp", None),
        P("dp", "rec", None, None, None),
    )
    return jax.shard_map(
        per_device, mesh=mesh, in_specs=in_specs, out_specs=out_specs, check_vma=False
    )
```

```python
import functools

import jax
import jax.numpy as jnp
from jax import lax
from jax.experimental import pallas as pl
from jax.experimental.pallas import tpu as pltpu
from jax.sharding import PartitionSpec as P

MESH = pl.DeviceIdType.MESH
TILE = 128

CHUNKS = (
    (0, 0, 0, 0, 8), (1, 0, 0, 0, 3), (0, 0, 0, 0, 6), (1, 0, 0, 0, 6), (0, 0, 0, 0, 6), (1, 1, 0, 0, 3), (0, 0, 0, 0, 5),
    (1, 0, 0, 0, 2), (0, 0, 0, 0, 6), (1, 1, 0, 0, 3), (0, 0, 0, 0, 3), (0, 1, 0, 0, 2), (1, 1, 0, 0, 1), (0, 1, 0, 1, 2),
)
BEGIN, ZSUM, YRELAY, YFINAL, ADAM, WEIGH, XRELAY, XFINAL, FINISH = range(9)
ORDER = (
    (BEGIN, 0), (BEGIN, 1), (BEGIN, 3), (ZSUM, 1), (YRELAY, 0), (YRELAY, 1),
    (BEGIN, 2), (YFINAL, 0), (YRELAY, 2), (BEGIN, 5), (ZSUM, 3), (ADAM, 1),
    (WEIGH, 1), (BEGIN, 4), (ADAM, 0), (YFINAL, 2), (BEGIN, 7), (XRELAY, 1),
    (BEGIN, 9), (WEIGH, 0), (YRELAY, 3), (YRELAY, 4), (XRELAY, 0), (ZSUM, 5),
    (BEGIN, 6), (ADAM, 2), (WEIGH, 2), (ADAM, 3), (WEIGH, 3), (YRELAY, 5),
    (YFINAL, 4), (BEGIN, 12), (XRELAY, 2), (YRELAY, 6), (XFINAL, 1), (XRELAY, 3),
    (BEGIN, 8), (ADAM, 4), (ADAM, 5), (YFINAL, 6), (WEIGH, 4), (XFINAL, 0),
    (YRELAY, 8), (XFINAL, 2), (WEIGH, 5), (ZSUM, 9), (BEGIN, 10), (XRELAY, 4),
    (ADAM, 6), (ZSUM, 12), (WEIGH, 6), (YFINAL, 8), (XFINAL, 3), (YRELAY, 9),
    (XRELAY, 5), (YRELAY, 10), (XFINAL, 4), (XRELAY, 6), (BEGIN, 11), (ADAM, 8),
    (BEGIN, 13), (WEIGH, 8), (YFINAL, 10), (YRELAY, 11), (ADAM, 9), (ZSUM, 7),
    (ADAM, 10), (YRELAY, 13), (XRELAY, 8), (XFINAL, 6), (FINISH, 4), (YRELAY, 12),
    (YFINAL, 11), (YRELAY, 7), (WEIGH, 10), (YFINAL, 13), (ADAM, 12), (WEIGH, 9),
    (ADAM, 7), (ADAM, 11), (WEIGH, 7), (ADAM, 13), (FINISH, 6), (FINISH, 1),
    (XFINAL, 8), (XRELAY, 10), (WEIGH, 12), (XRELAY, 7), (XRELAY, 9), (WEIGH, 11),
    (XFINAL, 10), (WEIGH, 13), (XFINAL, 5), (FINISH, 3), (FINISH, 0), (XRELAY, 12),
    (XFINAL, 7), (XFINAL, 9), (XRELAY, 11), (XFINAL, 12), (FINISH, 8), (FINISH, 2),
    (FINISH, 10), (FINISH, 7), (XFINAL, 13), (XFINAL, 11),
)

RELAY_UP, RELAY_DOWN, DIRECT_UP, DIRECT_DOWN, SECOND_UP, SECOND_DOWN = range(6)
TO_UP, TO_DOWN, TO_FAR = range(3)
Z_LO, CORE, X_RING, Z_HI, Z_HI_CORE = 6, 7, 8, 14, 15
SLOTS = 16
LOADS = 6
SETTLE = 16


def kernel(
    g_ref, p_ref, m_ref, v_ref, gen_ref,
    np_ref, nm_ref, nv_ref, par_ref,
    own, got, dif, cr, wgt, xr, hr,
    ssem, rsem, lsem,
):
    dp = lax.axis_index("dp")
    rec = lax.axis_index("rec")
    y, zl = dp // 2, dp % 2
    x, zh, core = rec // 4, (rec // 2) % 2, rec % 2
    y_up, y_down, y_far = (y + 1) % 4, (y + 3) % 4, (y + 2) % 4
    x_up, x_down, x_far = (x + 1) % 4, (x + 3) % 4, (x + 2) % 4
    to_y_up = (y_up * 2 + zl, rec)
    to_y_down = (y_down * 2 + zl, rec)
    to_y_far = (y_far * 2 + zl, rec)
    to_zl = (y * 2 + 1 - zl, rec)
    rec_core = x * 4 + zh * 2 + 1 - core
    rec_zh = x * 4 + (1 - zh) * 2 + core
    rec_both = x * 4 + (1 - zh) * 2 + 1 - core
    to_core, to_zh, to_both = (dp, rec_core), (dp, rec_zh), (dp, rec_both)
    to_x_up = (dp, x_up * 4 + zh * 2 + core)
    to_x_down = (dp, x_down * 4 + zh * 2 + core)

    to_x_far = (dp, x_far * 4 + zh * 2 + core)

    def z_first(k):
        return CHUNKS[k][0]

    def early(k):
        return CHUNKS[k][1]

    def y_direct(k):
        return CHUNKS[k][2]

    def x_direct(k):
        return CHUNKS[k][3]

    starts = []
    for _, _, _, _, tiles in CHUNKS:
        starts.append(starts[-1] + last if starts else 0)
        last = tiles * TILE

    def cols(k):
        return pl.ds(starts[k], CHUNKS[k][4] * TILE)

    def over_cols(k, work):
        start, tiles = starts[k], CHUNKS[k][4]
        step = 2 * TILE if tiles % 2 == 0 else TILE
        n = tiles * TILE // step
        if n == 1:
            work(pl.ds(start, step))
        else:
            def body(i, carry):
                work(pl.ds(pl.multiple_of(start + i * step, TILE), step))
                return carry

            lax.fori_loop(0, n, body, 0)

    def remote(k, slot, src, dst, device):
        return pltpu.make_async_remote_copy(
            src_ref=src, dst_ref=dst, send_sem=ssem.at[k, slot], recv_sem=rsem.at[k, slot],
            device_id=device, device_id_type=MESH,
        )

    def first_slots(direct):
        return (TO_UP, TO_DOWN, TO_FAR) if direct else (RELAY_UP, RELAY_DOWN, DIRECT_UP, DIRECT_DOWN)

    def y_place(k, slot):
        return (4 + slot // 2, (slot % 2) * 32, 32) if z_first(k) else (slot, 0, 64)

    def y_in(k, slot):
        if y_direct(k):
            return got.at[4 + slot, :, cols(k)] if z_first(k) else got.at[2 * slot:2 * slot + 2, :, cols(k)]
        i, r, n = y_place(k, slot)
        return got.at[i, pl.ds(r, n), cols(k)]

    def y_copy(k, slot):
        if y_direct(k):
            block = (y_up, y_down, y_far)[slot]
            src = got.at[block, :, cols(k)] if z_first(k) else g_ref.at[block, :, :, cols(k)]
            return remote(k, slot, src, y_in(k, slot), (to_y_up, to_y_down, to_y_far)[slot])

        def part(block, half):
            if z_first(k):
                return got.at[block, pl.ds(half * 32, 32), cols(k)]
            return g_ref.at[block, half, :, cols(k)]

        src = {
            RELAY_UP: lambda: part(y_far, 0),
            RELAY_DOWN: lambda: part(y_far, 1),
            DIRECT_UP: lambda: part(y_up, 1),
            DIRECT_DOWN: lambda: part(y_down, 0),
            SECOND_UP: lambda: y_in(k, RELAY_UP),
            SECOND_DOWN: lambda: y_in(k, RELAY_DOWN),
        }[slot]()
        return remote(k, slot, src, y_in(k, slot), to_y_up if slot % 2 == 0 else to_y_down)

    def zl_copy(k):
        if z_first(k):
            return remote(k, Z_LO, g_ref.at[:, 1 - zl, :, cols(k)], got.at[0:4, :, cols(k)], to_zl)
        return remote(k, Z_LO, own.at[1 - zl, :, cols(k)], got.at[6, :, cols(k)], to_zl)

    def group_copies(k):
        if early(k):
            return (
                remote(k, Z_HI_CORE, dif.at[1 - core, 1 - zh, :, :, cols(k)], cr.at[1, :, :, cols(k)], to_both),
                remote(k, Z_HI, dif.at[core, 1 - zh, :, :, cols(k)], hr.at[:, :, cols(k)], to_zh),
                remote(k, CORE, dif.at[1 - core, zh, :, :, cols(k)], cr.at[0, :, :, cols(k)], to_core),
            )
        return (remote(k, CORE, dif.at[1 - core, :, :, :, cols(k)], cr.at[:, :, :, cols(k)], to_core),)

    def x_part(k, block, half):
        if early(k):
            return wgt.at[block, 0, :, pl.ds(half * 8, 8), cols(k)]
        return wgt.at[block, half, :, :, cols(k)]

    def x_in(k, slot):
        if x_direct(k):
            return xr.at[2 * slot, :, :, cols(k)] if early(k) else xr.at[2 * slot:2 * slot + 2, :, :, cols(k)]
        return xr.at[slot, :, pl.ds(0, 8 if early(k) else 16), cols(k)]

    def x_copy(k, slot):
        if x_direct(k):
            block = (x_up, x_down, x_far)[slot]
            src = wgt.at[block, 0, :, :, cols(k)] if early(k) else wgt.at[block, :, :, :, cols(k)]
            return remote(k, X_RING + slot, src, x_in(k, slot), (to_x_up, to_x_down, to_x_far)[slot])

        src = {
            RELAY_UP: lambda: x_part(k, x_far, 0),
            RELAY_DOWN: lambda: x_part(k, x_far, 1),
            DIRECT_UP: lambda: x_part(k, x_up, 1),
            DIRECT_DOWN: lambda: x_part(k, x_down, 0),
            SECOND_UP: lambda: x_in(k, RELAY_UP),
            SECOND_DOWN: lambda: x_in(k, RELAY_DOWN),
        }[slot]()
        return remote(k, X_RING + slot, src, x_in(k, slot), to_x_up if slot % 2 == 0 else to_x_down)

    def zh_copy(k):
        return remote(k, Z_HI, wgt.at[x, 1 - zh, :, :, cols(k)], hr.at[:, :, cols(k)], to_zh)

    def arrived(k, slot, buf):
        remote(k, slot, buf, buf, to_core).wait_recv()

    def loads(k):
        c = cols(k)
        if z_first(k):
            pairs = [(g_ref.at[:, zl, :, c], own.at[:, :, c])]
        elif y_direct(k):
            pairs = [(g_ref.at[y, :, :, c], own.at[0:2, :, c])]
        else:
            pairs = [
                (g_ref.at[y_up, 0, :, c], own.at[2, :, c]),
                (g_ref.at[y_down, 1, :, c], own.at[3, :, c]),
                (g_ref.at[y, :, :, c], own.at[0:2, :, c]),
            ]
        state = ((p_ref, np_ref), (m_ref, nm_ref), (v_ref, nv_ref))
        pairs += [(src.at[0, :, c], dst.at[0, :, c]) for src, dst in state]
        return [functools.partial(pltpu.make_async_copy, src, dst, lsem.at[k, i]) for i, (src, dst) in enumerate(pairs)]

    loaded = []

    def begin(k):
        if z_first(k):
            zl_copy(k).start()
        else:
            for slot in first_slots(y_direct(k)):
                y_copy(k, slot).start()
        if k not in loaded:
            for copy in loads(k):
                copy().start()

    def zsum(k):
        loads(k)[0]().wait()
        arrived(k, Z_LO, got.at[0:4, :, cols(k)])

        def add(block):
            def work(c):
                got[block, :, c] = got[block, :, c] + own[block, :, c]

            over_cols(k, work)

        if y_direct(k):
            for slot, block in ((TO_FAR, y_far), (TO_UP, y_up), (TO_DOWN, y_down)):
                add(block)
                y_copy(k, slot).start()
        else:
            add(y_far)
            y_copy(k, RELAY_UP).start()
            y_copy(k, RELAY_DOWN).start()
            add(y_up)
            y_copy(k, DIRECT_UP).start()
            add(y_down)
            y_copy(k, DIRECT_DOWN).start()
        add(y)

    def yrelay(k):
        for slot, block, onward in ((RELAY_UP, y_up, SECOND_UP), (RELAY_DOWN, y_down, SECOND_DOWN)):
            if not z_first(k):
                loads(k)[slot]().wait()
            arrived(k, slot, y_in(k, slot))
            i, r, n = y_place(k, slot)

            def work(c):
                if z_first(k):
                    mine = got[block, pl.ds(slot * 32, 32), c]
                else:
                    mine = own[2 + slot, :, c]
                got[i, pl.ds(r, n), c] = got[i, pl.ds(r, n), c] + mine

            over_cols(k, work)
            y_copy(k, onward).start()

    def yfinal(k):
        loads(k)[0 if y_direct(k) else 2]().wait()
        if y_direct(k):
            for slot in range(3):
                arrived(k, slot, y_in(k, slot))
        for turn, half in enumerate((1 - zl, zl)):
            if not y_direct(k):
                for slot in (3 - half, 4 + half):
                    arrived(k, slot, got.at[slot, :, cols(k)])

            def work(c):
                if y_direct(k):
                    own[half, :, c] = own[half, :, c] + got[half, :, c] + got[2 + half, :, c] + got[4 + half, :, c]
                else:
                    own[half, :, c] = own[half, :, c] + got[3 - half, :, c] + got[4 + half, :, c]

            over_cols(k, work)
            if turn == 0:
                zl_copy(k).start()

    def adam(k):
        for copy in loads(k)[-3:]:
            copy().wait()
        if z_first(k):
            for slot in range(3) if y_direct(k) else (DIRECT_DOWN, SECOND_UP, DIRECT_UP, SECOND_DOWN):
                arrived(k, slot, y_in(k, slot))
        else:
            arrived(k, Z_LO, got.at[6, :, cols(k)])
        bias_one = 1.0 - 0.9**10
        bias_two = 1.0 - 0.999**10

        def work(c):
            for q in range(4):
                r = pl.ds(q * 16, 16)
                if z_first(k) and y_direct(k):
                    grad = got[y, r, c] + got[4, r, c] + got[5, r, c] + got[6, r, c]
                elif z_first(k):
                    grad = got[y, r, c]
                    for slot in ((DIRECT_DOWN, SECOND_UP) if q < 2 else (DIRECT_UP, SECOND_DOWN)):
                        i, first_row, _ = y_place(k, slot)
                        grad = grad + got[i, pl.ds(first_row + (q % 2) * 16, 16), c]
                else:
                    grad = own[zl, r, c] + got[6, r, c]
                params, first, second = np_ref[0, r, c], nm_ref[0, r, c], nv_ref[0, r, c]
                square = grad * grad
                new_first = 0.9 * first + 0.1 * grad
                new_second = 0.999 * second + 0.001 * square
                step = new_first / bias_one / (jnp.sqrt(new_second / bias_two) + 1e-08) + 0.1 * params
                dif[q % 2, q // 2, 0, :, c] = step
                dif[q % 2, q // 2, 1, :, c] = grad - first
                dif[q % 2, q // 2, 2, :, c] = square - second
                np_ref[0, r, c] = params - 0.001 * step
                nm_ref[0, r, c] = new_first
                nv_ref[0, r, c] = new_second

        over_cols(k, work)
        for copy in group_copies(k):
            copy.start()

    def weigh(k):
        if early(k):
            arrived(k, CORE, cr.at[0, :, :, cols(k)])
            arrived(k, Z_HI, hr.at[:, :, cols(k)])
            arrived(k, Z_HI_CORE, cr.at[1, :, :, cols(k)])
        else:
            arrived(k, CORE, cr.at[:, :, :, cols(k)])

        def work(c):
            if early(k):
                fields = (dif[core, zh, :, :, c], cr[0, :, :, c], hr[:, :, c], cr[1, :, :, c])
                for j in range(4):
                    total = gen_ref[j, rec] * fields[0]
                    for member, field in zip((rec_core, rec_zh, rec_both), fields[1:]):
                        total = total + gen_ref[j, member] * field
                    wgt[j, 0, :, :, c] = total
            else:
                for half in range(2):
                    mine, other = dif[core, half, :, :, c], cr[half, :, :, c]
                    for j in range(4):
                        wgt[j, half, :, :, c] = gen_ref[j, rec] * mine + gen_ref[j, rec_core] * other

        over_cols(k, work)
        for slot in first_slots(x_direct(k)):
            x_copy(k, slot).start()

    def xrelay(k):
        for slot, block, onward in ((RELAY_UP, x_up, SECOND_UP), (RELAY_DOWN, x_down, SECOND_DOWN)):
            arrived(k, X_RING + slot, x_in(k, slot))

            def work(c):
                if early(k):
                    r = pl.ds(0, 8)
                    xr[slot, :, r, c] = xr[slot, :, r, c] + wgt[block, 0, :, pl.ds(slot * 8, 8), c]
                else:
                    xr[slot, :, :, c] = xr[slot, :, :, c] + wgt[block, slot, :, :, c]

            over_cols(k, work)
            x_copy(k, onward).start()

    def xfinal(k):
        if x_direct(k):
            for slot in range(3):
                arrived(k, X_RING + slot, x_in(k, slot))

            def total(half, c):
                return wgt[x, half, :, :, c] + xr[half, :, :, c] + xr[2 + half, :, :, c] + xr[4 + half, :, :, c]

            if early(k):
                def work(c):
                    par_ref[0, 0, :, :, c] = total(0, c)

                over_cols(k, work)
                return
            for turn, half in enumerate((1 - zh, zh)):
                def work(c):
                    wgt[x, half, :, :, c] = total(half, c)

                over_cols(k, work)
                if turn == 0:
                    zh_copy(k).start()
            return
        if early(k):
            for slot in (DIRECT_DOWN, SECOND_UP, DIRECT_UP, SECOND_DOWN):
                arrived(k, X_RING + slot, x_in(k, slot))

            def work(c):
                r = pl.ds(0, 8)
                for half in range(2):
                    h = pl.ds(half * 8, 8)
                    par_ref[0, 0, :, h, c] = wgt[x, 0, :, h, c] + xr[3 - half, :, r, c] + xr[4 + half, :, r, c]

            over_cols(k, work)
            return
        for turn, half in enumerate((1 - zh, zh)):
            for slot in (3 - half, 4 + half):
                arrived(k, X_RING + slot, xr.at[slot, :, :, cols(k)])

            def work(c):
                wgt[x, half, :, :, c] = wgt[x, half, :, :, c] + xr[3 - half, :, :, c] + xr[4 + half, :, :, c]

            over_cols(k, work)
            if turn == 0:
                zh_copy(k).start()

    def finish(k):
        arrived(k, Z_HI, hr.at[:, :, cols(k)])

        def work(c):
            par_ref[0, 0, :, :, c] = wgt[x, zh, :, :, c] + hr[:, :, c]

        over_cols(k, work)

    def gradient_sent(k):
        for slot in range(3 if y_direct(k) else 6):
            y_copy(k, slot).wait_send()
        zl_copy(k).wait_send()

    def parity_sent(k):
        for copy in group_copies(k):
            copy.wait_send()
        for slot in range(3 if x_direct(k) else 6):
            x_copy(k, slot).wait_send()
        if not early(k):
            zh_copy(k).wait_send()

    stages = {
        BEGIN: begin, ZSUM: zsum, YRELAY: yrelay, YFINAL: yfinal, ADAM: adam,
        WEIGH: weigh, XRELAY: xrelay, XFINAL: xfinal, FINISH: finish,
    }
    barrier = pltpu.get_barrier_semaphore()
    peers = [to_y_up, to_y_down, to_zl, to_core, to_zh, to_x_up, to_x_down]
    peers += [to_both] if any(early(k) for k in range(len(CHUNKS))) else []
    peers += [to_y_far] if any(y_direct(k) for k in range(len(CHUNKS))) else []
    peers += [to_x_far] if any(x_direct(k) for k in range(len(CHUNKS))) else []
    for peer in peers:
        pl.semaphore_signal(barrier, inc=1, device_id=peer, device_id_type=MESH)
    for stage, k in ORDER:
        if stage != BEGIN:
            break
        loaded.append(k)
        for copy in loads(k):
            copy().start()
    pl.semaphore_wait(barrier, len(peers))

    last = {k: at for at, (_, k) in enumerate(ORDER)}
    for at, (stage, k) in enumerate(ORDER):
        stages[stage](k)
        if stage == WEIGH:
            gradient_sent(k)
        for j in range(len(CHUNKS)):
            if last[j] + SETTLE == at:
                parity_sent(j)
    for j in range(len(CHUNKS)):
        if last[j] + SETTLE >= len(ORDER):
            parity_sent(j)


def copy_out(*refs):
    n = len(refs) // 2
    sems = refs[-1]
    copies = []
    for i in range(4):
        src, dst = refs[i], refs[4 + i]
        for part in range(4):
            if i < 3:
                where = (0, pl.ds(part * 16, 16))
            elif part < 3:
                where = (0, 0, part)
            else:
                continue
            copies.append(pltpu.make_async_copy(src.at[where], dst.at[where], sems.at[i, part]))
    for copy in copies:
        copy.start()
    for copy in copies:
        copy.wait()


def per_device(grad_parts, params, first_moment, second_moment, generator):
    width = params.shape[2]
    assert sum(tiles for _, _, _, _, tiles in CHUNKS) * TILE == width
    n = len(CHUNKS)
    any_spec = pl.BlockSpec(memory_space=pl.ANY)
    f32 = jnp.float32
    outs = (jax.ShapeDtypeStruct(params.shape, f32),) * 3 + (jax.ShapeDtypeStruct((1, 1, 3, 16, width), f32),)
    results = pl.pallas_call(
        kernel,
        out_shape=tuple(pltpu.VMEM(out.shape, out.dtype) for out in outs),
        in_specs=[any_spec] * 4 + [pl.BlockSpec(memory_space=pltpu.SMEM)],
        out_specs=(pl.BlockSpec(memory_space=pltpu.VMEM),) * 4,
        scratch_shapes=[
            pltpu.VMEM((4, 64, width), f32),
            pltpu.VMEM((7, 64, width), f32),
            pltpu.VMEM((2, 2, 3, 16, width), f32),
            pltpu.VMEM((2, 3, 16, width), f32),
            pltpu.VMEM((4, 2, 3, 16, width), f32),
            pltpu.VMEM((6, 3, 16, width), f32),
            pltpu.VMEM((3, 16, width), f32),
            pltpu.SemaphoreType.DMA((n, SLOTS)),
            pltpu.SemaphoreType.DMA((n, SLOTS)),
            pltpu.SemaphoreType.DMA((n, LOADS)),
        ],
        compiler_params=pltpu.CompilerParams(
            collective_id=0, has_side_effects=True, vmem_limit_bytes=50 << 20
        ),
        cost_estimate=pl.CostEstimate(
            flops=100_000_000, bytes_accessed=60_000_000, transcendentals=458_752
        ),
        name="adam_parity",
    )(grad_parts.reshape(4, 2, 64, width), params, first_moment, second_moment, generator)
    return pl.pallas_call(
        copy_out,
        out_shape=outs,
        in_specs=[any_spec] * 4,
        out_specs=(any_spec,) * 4,
        scratch_shapes=[pltpu.SemaphoreType.DMA((4, 4))],
        compiler_params=pltpu.CompilerParams(vmem_limit_bytes=1 << 20),
        cost_estimate=pl.CostEstimate(flops=0, bytes_accessed=13_800_000, transcendentals=0),
        name="copy_out",
    )(*results)


def solution(mesh):
    in_specs = (
        P("dp", "rec", None, None),
        P("rec", "dp", None),
        P("rec", "dp", None),
        P("rec", "dp", None),
        P(),
    )
    out_specs = (
        P("rec", "dp", None),
        P("rec", "dp", None),
        P("rec", "dp", None),
        P("dp", "rec", None, None, None),
    )
    return jax.shard_map(
        per_device, mesh=mesh, in_specs=in_specs, out_specs=out_specs, check_vma=False
    )
```
